128 devices in a mesh: space: 32 (over x, y, core), rank: 4 (over z).
Axes of the slice: x: 4, y: 4, z: 4, core: 2. Of those that a mesh axis runs over, the one named last changes fastest.
Arguments:
- xfactor: float32 [128, 524288], P('rank', 'space'), may hold values from -6 to 6
- volume: float32 [3, 64, 64], replicated, may hold values from -0.75 to 0.75
- upwind: float32 [3, 64, 64], replicated, may hold values from -0.75 to 0.75
- neighbor: int32 [3, 8192], P(None, 'space'), may hold values from -1 to 8190, as said below
- coeffs: float32 [512, 128], replicated, may hold values from -0.25 to 0.25
Outputs:
- new_factor: float32 [128, 524288], P(None, ('space', 'rank'))
- r_factor: float32 [512, 512], replicated
The draws below stay inside these ranges and needn't reach their ends.
Inputs may be any that keep to these rules, and one draw needn't show every extreme that they name: neighbor[d, e] is -1 or an element between e - 32 and e - 1; the distance 32 occurs in every direction.
All inputs are finite; a program needn't handle non-finite values.
Results may differ from the reference program's by a relative error of at most 0.0001.
Values sent between devices are 32-bit elements; how exact they have to be, the bound alone decides.
No kernel may reach another device: no remote copies, remote signals or barrier semaphores. Data moves between devices by JAX's collectives and lax.ppermute only.
A program may use at most 128 MiB of HBM per device.

```python
import jax
import jax.numpy as jnp
from jax import lax

NODES = 64
R = 128
HALO_EL = 32
NEL = 8192
NX = 524288
CAND = 512
COLS_DEV = 32


def draw_neighbor(key, part):
    offsets = jax.random.randint(key, (3, NEL), 1, HALO_EL + 1)
    offsets = offsets.at[:, NEL - 1].set(1)
    offsets = offsets.at[:, NEL - 2].set(HALO_EL)
    elements = jnp.arange(NEL, dtype=jnp.int32)[None, :]
    target = elements - offsets
    return jnp.where(target >= 0, target, -1).astype(jnp.int32)


def block_levels(own_key, dims, split, low, largest):
    factor_of, own = 1.0, jax.random.fold_in(own_key, 6)
    for axis_at, blocks in split:
        draws = jnp.exp(jax.random.uniform(jax.random.fold_in(own, axis_at), (blocks,), jnp.float32, low / len(split), largest / len(split)))
        factor_of = factor_of * jnp.repeat(draws, dims[axis_at] // blocks).reshape([-1 if axis == axis_at else 1 for axis in range(len(dims))])
    return factor_of


def gaussian(key, dims, deviation, limit, pieces=(), held_as=jnp.bfloat16):
    values = jax.random.normal(key, dims, jnp.float32) * deviation
    if len(pieces) > 0:
        values = block_levels(key, dims, pieces, -0.22, 0.18) * values
    return jnp.clip(values, min=-limit, max=limit).astype(held_as)


def setup_inputs(seed: int = 0) -> dict:
    streams_of = jax.random.split(jax.random.key(seed), 6)
    xfactor = gaussian(streams_of[0], (R, NX), 1.0, 6.0, ((0, 4), (1, 32)), jnp.float32)
    volume = gaussian(streams_of[1], (3, NODES, NODES), NODES ** -0.5, 0.75, (), jnp.float32)
    upwind = gaussian(streams_of[2], (3, NODES, NODES), NODES ** -0.5, 0.75, (), jnp.float32)
    neighbor = draw_neighbor(jax.random.fold_in(streams_of[5], 71), 0)
    coeffs = gaussian(streams_of[4], (CAND, R), CAND ** -0.5, 0.25, (), jnp.float32)
    return {"xfactor": xfactor, "volume": volume, "upwind": upwind, "neighbor": neighbor, "coeffs": coeffs}


def moved_all(xfactor, volume, upwind, neighbor):
    blocks = xfactor.reshape(R, NEL, NODES)
    result = []
    for direc in range(3):
        valid = neighbor[direc] >= 0
        index = jnp.where(valid, neighbor[direc], 0).astype(jnp.int32)
        neigh = jnp.take(blocks, index, axis=1) * valid.astype(jnp.float32)[None, :, None]
        here = jnp.einsum('ij,cej->cei', volume[direc], blocks, precision=lax.Precision.HIGHEST)
        there = jnp.einsum('ij,cej->cei', upwind[direc], neigh, precision=lax.Precision.HIGHEST)
        result.append((here + there).reshape(R, NX))
    return result

def reference(xfactor, volume, upwind, neighbor, coeffs):
    moved = moved_all(xfactor, volume, upwind, neighbor)
    stacked = jnp.stack([xfactor] + moved, axis=0)
    quarters = R // COLS_DEV
    stacked = stacked.reshape(4, quarters, COLS_DEV, NX)
    candidate = jnp.transpose(stacked, (1, 0, 2, 3)).reshape(CAND, NX)
    gram = jnp.dot(candidate, candidate.T, precision=lax.Precision.HIGHEST) / NX
    lower = jnp.linalg.cholesky(gram)
    basis = jax.scipy.linalg.solve_triangular(lower, candidate, lower=True)
    new_factor = jnp.dot(coeffs.T, basis, precision=lax.Precision.HIGHEST)
    return (new_factor, lower.T)
```

```python
import jax
import jax.numpy as jnp
from jax import lax
from jax.experimental import pallas as pl
from jax.experimental.pallas import tpu as pltpu
from jax.sharding import Mesh
from jax.sharding import PartitionSpec as P

SPACE_RANK = ("x", "y", "core", "rank")
SPACE = ("x", "y", "core")
HALO_EL = 32
F32, BF16 = jnp.float32, jnp.bfloat16
VMEM = pl.BlockSpec(memory_space=pltpu.VMEM)
SMEM = pl.BlockSpec(memory_space=pltpu.SMEM)
ANY = pl.BlockSpec(memory_space=pl.ANY)


def halves(x):
    high = x.astype(BF16)
    return high, (x - high.astype(F32)).astype(BF16)


def product(a, b, over):
    dims = (((over[0],), (over[1],)), ((), ()))
    return lax.dot_general(a, b, dims, preferred_element_type=F32)


def exact(a, b, over):
    dims = (((over[0],), (over[1],)), ((), ()))
    return lax.dot_general(
        a, b, dims, precision=lax.Precision.HIGHEST, preferred_element_type=F32
    )


TILES = 48
ZERO_TILE = 2 * TILES


def transport_kernel(
    place, index, m0, m1, m2, m3, h0, h1, h2, h3, mats,
    gram, cand_high, cand_low,
    mats_high, mats_low, tiles_high, tiles_low, lhs_high, lhs_low, c_high, c_low, same, cross, sems,
):
    mats_high[...], mats_low[...] = halves(mats[...])
    tiles_high[ZERO_TILE] = jnp.zeros((128, 128), BF16)
    tiles_low[ZERO_TILE] = jnp.zeros((128, 128), BF16)
    for piece, (main, halo) in enumerate(((m0, h0), (m1, h1), (m2, h2), (m3, h3))):
        rows = pl.ds(pl.multiple_of(place[piece] * 32, 32), 32)
        values = jnp.concatenate([halo[...], main[...]], axis=1)
        for base, array in ((0, values), (TILES, pltpu.roll(values, 64, 1))):
            for tile in range(TILES):
                high, low = halves(array[:, 128 * tile : 128 * tile + 128])
                tiles_high[base + tile, rows, :] = high
                tiles_low[base + tile, rows, :] = low
    lower = lax.broadcasted_iota(jnp.int32, (128, 128), 1) < 64
    same[...] = jnp.zeros_like(same)
    cross[...] = jnp.zeros_like(cross)

    def out_copies(chunk):
        lanes = pl.ds(pl.multiple_of(chunk * 1024, 1024), 1024)
        return (
            pltpu.make_async_copy(c_high.at[:, lanes], cand_high.at[:, lanes], sems.at[0]),
            pltpu.make_async_copy(c_low.at[:, lanes], cand_low.at[:, lanes], sems.at[1]),
        )

    @pl.loop(0, 4)
    def _(chunk):
        for tiles, lhs, cand in ((tiles_high, lhs_high, c_high), (tiles_low, lhs_low, c_low)):
            for pair in range(8):
                tile = tiles[HALO_EL // 2 + chunk * 8 + pair]
                lhs[pair // 2, :, 128 * (pair % 2) : 128 * (pair % 2) + 128] = tile
                lanes = pl.ds(pl.multiple_of(chunk * 1024 + pair * 128, 128), 128)
                for q in range(4):
                    cand[128 * q : 128 * q + 32, lanes] = tile[32 * q : 32 * q + 32]
        for direc in range(3):
            for pair in range(8):
                first = index[direc, chunk * 16 + 2 * pair]
                second = index[direc, chunk * 16 + 2 * pair + 1]
                at = 256 + 128 * (pair % 2)
                for tiles, lhs in ((tiles_high, lhs_high), (tiles_low, lhs_low)):
                    lhs[pair // 2, :, at : at + 128] = jnp.where(lower, tiles[first], tiles[second])
            high = lhs_high[...].reshape(512, 512)
            low = lhs_low[...].reshape(512, 512)
            moved = product(high, mats_high[direc], (1, 0)) + (
                product(low, mats_high[direc], (1, 0)) + product(high, mats_low[direc], (1, 0))
            )
            parts = halves(moved)
            for group in range(4):
                lanes = pl.ds(pl.multiple_of(chunk * 1024 + group * 256, 256), 256)
                for q in range(4):
                    to = 128 * q + 32 * (direc + 1)
                    rows = slice(128 * group + 32 * q, 128 * group + 32 * q + 32)
                    c_high[to : to + 32, lanes] = parts[0][rows]
                    c_low[to : to + 32, lanes] = parts[1][rows]
        for copy in out_copies(chunk):
            copy.start()
        lanes = pl.ds(pl.multiple_of(chunk * 1024, 1024), 1024)
        high, low = c_high[:, lanes], c_low[:, lanes]
        same[0:256, :] += product(high[0:256], high, (1, 1))
        same[256:512, 256:512] += product(high[256:512], high[256:512], (1, 1))
        cross[...] += product(high, low, (1, 1))

    spot = 0
    for a in range(4):
        for b in range(a, 4):
            rows, cols = slice(128 * a, 128 * a + 128), slice(128 * b, 128 * b + 128)
            total = same[rows, cols] + (cross[rows, cols] + cross[cols, rows].T)
            gram[128 * spot : 128 * spot + 128, :] = total * (1.0 / 524288)
            spot += 1

    @pl.loop(0, 4)
    def _(chunk):
        for copy in out_copies(chunk):
            copy.wait()


def transported(place, index, mains, halos, mats):
    big = jax.ShapeDtypeStruct((512, 4096), BF16)
    return pl.pallas_call(
        transport_kernel,
        out_shape=(jax.ShapeDtypeStruct((1280, 128), F32), big, big),
        in_specs=[SMEM, SMEM] + [VMEM] * 9,
        out_specs=(VMEM, ANY, ANY),
        scratch_shapes=[
            pltpu.VMEM((3, 512, 256), BF16),
            pltpu.VMEM((3, 512, 256), BF16),
            pltpu.VMEM((2 * TILES + 1, 128, 128), BF16),
            pltpu.VMEM((2 * TILES + 1, 128, 128), BF16),
            pltpu.VMEM((4, 128, 512), BF16),
            pltpu.VMEM((4, 128, 512), BF16),
            pltpu.VMEM((512, 4096), BF16),
            pltpu.VMEM((512, 4096), BF16),
            pltpu.VMEM((512, 512), F32),
            pltpu.VMEM((512, 512), F32),
            pltpu.SemaphoreType.DMA((2,)),
        ],
        compiler_params=pltpu.CompilerParams(vmem_limit_bytes=48 << 20),
        name="transport",
    )(place, index, *mains, *halos, mats)


def along_lanes(x, lane):
    return jnp.broadcast_to(x[:, lane : lane + 1], (8, 128))


def along_rows(x, row):
    return jnp.broadcast_to(x[row : row + 1, :], (8, 128))


def factor_block(left, right):
    row = lax.broadcasted_iota(jnp.int32, (8, 128), 0)
    left, right = list(left), list(right)
    upper, inverse = [], []
    for step in range(16):
        c = [[along_lanes(left[i], 8 * step + l) for i in range(step, 16)] for l in range(8)]
        s = [[along_rows(c[l][0], i) if i >= l else None for l in range(8)] for i in range(8)]
        t = [[None] * 8 for _ in range(8)]
        for j in range(8):
            r = lax.rsqrt(s[j][j])
            t[j][j] = r
            for i in range(j + 1, 8):
                s[i][j] = s[i][j] * r
            for l in range(j + 1, 8):
                for i in range(l, 8):
                    s[i][l] = s[i][l] - s[i][j] * s[l][j]
            for l in range(j):
                total = s[j][l] * t[l][l]
                for m in range(l + 1, j):
                    total = total + s[j][m] * t[m][l]
                t[j][l] = -(total * r)

        def combined(lines, j, t=t):
            total = t[j][0] * lines[0]
            for l in range(1, j + 1):
                total = total + t[j][l] * lines[l]
            return total

        def packed(lines):
            out = lines[0]
            for j in range(1, 8):
                out = jnp.where(row == j, lines[j], out)
            return out

        lines = [along_rows(left[step], l) for l in range(8)]
        wide_left = [combined(lines, j) for j in range(8)]
        lines = [along_rows(right[step], l) for l in range(8)]
        wide_right = [combined(lines, j) for j in range(8)]
        upper.append(packed(wide_left))
        inverse.append(packed(wide_right))
        for i in range(step + 1, 16):
            lines = [c[l][i - step] for l in range(8)]
            for j in range(8):
                factor = combined(lines, j)
                left[i] = left[i] - factor * wide_left[j]
                right[i] = right[i] - factor * wide_right[j]
    return upper, inverse


def factor_kernel(gram, coeffs, cand_high, cand_low, r_out, new_out, work, c_high, c_low, sems):
    copies = (
        pltpu.make_async_copy(cand_high, c_high, sems.at[0]),
        pltpu.make_async_copy(cand_low, c_low, sems.at[1]),
    )
    for copy in copies:
        copy.start()
    row = lax.broadcasted_iota(jnp.int32, (128, 128), 0)
    col = lax.broadcasted_iota(jnp.int32, (128, 128), 1)
    eye = (row == col).astype(F32)
    zero = jnp.zeros((128, 128), F32)
    at = [slice(128 * a, 128 * a + 128) for a in range(4)]
    beside = [slice(512 + 128 * a, 640 + 128 * a) for a in range(4)]
    spot = 0
    for a in range(4):
        for b in range(4):
            work[at[a], beside[b]] = eye if a == b else zero
            if b >= a:
                work[at[a], at[b]] = gram[128 * spot : 128 * spot + 128, :]
                spot += 1
            else:
                r_out[at[a], at[b]] = zero
    for a in range(4):
        first = 128 * a
        upper, inverse = factor_block(
            [work[first + 8 * i : first + 8 * i + 8, at[a]] for i in range(16)],
            [eye[8 * i : 8 * i + 8] for i in range(16)],
        )
        diag = jnp.where(row >= col, jnp.concatenate(inverse, axis=0), 0.0)
        r_out[at[a], at[a]] = jnp.where(row <= col, jnp.concatenate(upper, axis=0), 0.0)
        work[at[a], beside[a]] = diag
        if a:
            done = slice(512, 512 + first)
            work[at[a], done] = exact(diag, work[at[a], done], (1, 0))
        if a < 3:
            rest = exact(diag, work[at[a], first + 128 : 512], (1, 0))
            r_out[at[a], first + 128 : 512] = rest
            for b in range(a + 1, 4):
                mine = rest[:, 128 * (b - a - 1) : 128 * (b - a)]
                right = slice(128 * b, 512)
                work[at[b], right] -= exact(mine, rest[:, 128 * (b - a - 1) :], (0, 0))
                done = slice(512, 512 + first + 128)
                work[at[b], done] -= exact(mine, work[at[a], done], (0, 0))
    weight_high, weight_low = halves(exact(coeffs[...], work[:, 512:1024], (0, 0)))
    for copy in copies:
        copy.wait()

    @pl.loop(0, 8)
    def _(chunk):
        lanes = pl.ds(pl.multiple_of(chunk * 512, 512), 512)
        high, low = c_high[:, lanes], c_low[:, lanes]
        new_out[:, lanes] = product(weight_high, high, (1, 0)) + (
            product(weight_high, low, (1, 0)) + product(weight_low, high, (1, 0))
        )


def factored(gram, coeffs, cand_high, cand_low):
    return pl.pallas_call(
        factor_kernel,
        out_shape=(
            jax.ShapeDtypeStruct((512, 512), F32),
            jax.ShapeDtypeStruct((128, 4096), F32),
        ),
        in_specs=[VMEM, VMEM, ANY, ANY],
        out_specs=(VMEM, VMEM),
        scratch_shapes=[
            pltpu.VMEM((512, 1024), F32),
            pltpu.VMEM((512, 4096), BF16),
            pltpu.VMEM((512, 4096), BF16),
            pltpu.SemaphoreType.DMA((2,)),
        ],
        compiler_params=pltpu.CompilerParams(vmem_limit_bytes=48 << 20),
        name="factor",
    )(gram, coeffs, cand_high, cand_low)


def sent(value, axis, by):
    count = lax.axis_size(axis)
    return lax.ppermute(value, axis, [(i, (i + by) % count) for i in range(count)])


def pieces_from_here(value, axis):
    count, here = lax.axis_size(axis), lax.axis_index(axis)
    split = value.reshape(count, -1, value.shape[-1])
    return [
        lax.dynamic_index_in_dim(split, (here + by) % count, 0, keepdims=False)
        for by in range(count)
    ]


def scattered_sum(value, axis):
    pieces = pieces_from_here(value, axis)
    return sum((sent(pieces[by], axis, by) for by in range(1, len(pieces))), pieces[0])


def exchanged_sum(value, axis):
    one, two, three = (sent(value, axis, by) for by in range(1, 4))
    return (value + two) + (one + three)


def gathered(value, axis):
    count, here = lax.axis_size(axis), lax.axis_index(axis)
    out = jnp.zeros((count, *value.shape), value.dtype)
    for by in range(count):
        part = sent(value, axis, by) if by else value
        out = lax.dynamic_update_index_in_dim(out, part, (here - by) % count, 0)
    return out.reshape(-1, value.shape[-1])


def summed(gram):
    part = scattered_sum(scattered_sum(gram, "core"), "x")
    part = exchanged_sum(exchanged_sum(part, "y"), "rank")
    return gathered(gathered(part, "x"), "core")


def tile_index(neighbor, first):
    at = neighbor - first
    odd_place = jnp.arange(neighbor.shape[1]) % 2
    tile = jnp.where(at % 2 == odd_place, at // 2, TILES + (at + 1) // 2)
    return jnp.where(neighbor >= 0, tile, ZERO_TILE).astype(jnp.int32)


def shards(xfactor, volume, upwind, neighbor, coeffs):
    sub_rows = xfactor.shape[1] // 4
    half = sub_rows // 2
    sub_elems = neighbor.shape[1] // 4
    rank = lax.axis_index("rank")
    count = lax.axis_size(SPACE)
    tail = xfactor[:, 3 * sub_rows + half :]
    above = lax.ppermute(tail, SPACE, [(i, i + 1) for i in range(count - 1)])
    mains, halos = [], []
    for by in range(4):
        to = (rank + by) % 4
        piece = lax.dynamic_slice_in_dim(xfactor, to * sub_rows, sub_rows, 1)
        mains.append(sent(piece, "rank", by) if by else piece)
    for by in range(4):
        to = (rank + by) % 4
        inside = lax.dynamic_slice_in_dim(xfactor, jnp.maximum(to * sub_rows - half, 0), half, 1)
        piece = jnp.where(to == 0, above, inside)
        halos.append(sent(piece, "rank", by) if by else piece)
    place = jnp.stack([(rank - by) % 4 for by in range(4)]).astype(jnp.int32)
    first = (lax.axis_index(SPACE) * 4 + rank) * sub_elems - HALO_EL
    own = lax.dynamic_slice_in_dim(neighbor, rank * sub_elems, sub_elems, 1)
    four = jnp.eye(4, dtype=F32)
    mats = jnp.stack([volume, upwind], axis=1)
    mats = jnp.einsum("ab,dkij->dkajbi", four, mats, precision=lax.Precision.HIGHEST)
    gram, cand_high, cand_low = transported(
        place, tile_index(own, first), mains, halos, mats.reshape(3, 512, 256)
    )
    r_factor, new_factor = factored(summed(gram), coeffs, cand_high, cand_low)
    return new_factor, r_factor


def solution(mesh):
    finer = Mesh(mesh.devices.reshape(4, 4, 2, 4), SPACE_RANK)
    placed = (P("rank", SPACE), P(), P(), P(None, SPACE), P())
    return jax.shard_map(
        shards, mesh=finer, in_specs=placed, out_specs=(P(None, SPACE_RANK), P()), check_vma=False
    )
```

```python
import functools

import jax
import jax.numpy as jnp
from jax import lax
from jax.experimental import pallas as pl
from jax.experimental.pallas import tpu as pltpu
from jax.sharding import Mesh
from jax.sharding import PartitionSpec as P

SPACE_RANK = ("x", "y", "core", "rank")
SPACE = ("x", "y", "core")
HALO_EL = 32
F32, BF16 = jnp.float32, jnp.bfloat16
VMEM = pl.BlockSpec(memory_space=pltpu.VMEM)
SMEM = pl.BlockSpec(memory_space=pltpu.SMEM)
ANY = pl.BlockSpec(memory_space=pl.ANY)


def halves(x):
    high = x.astype(BF16)
    return high, (x - high.astype(F32)).astype(BF16)


def product(a, b, over):
    dims = (((over[0],), (over[1],)), ((), ()))
    return lax.dot_general(a, b, dims, preferred_element_type=F32)


def exact(a, b, over):
    dims = (((over[0],), (over[1],)), ((), ()))
    return lax.dot_general(
        a, b, dims, precision=lax.Precision.HIGHEST, preferred_element_type=F32
    )


TILES = 32
ZERO_TILE = 2 * TILES
WIDE = 2048


def transport_kernel(second, place, index, xfactor, *refs):
    mains, refs = refs[:3], refs[3:]
    above, refs = ((), refs) if second else (refs[:4], refs[4:])
    before, refs = (None, refs) if second else (refs[0], refs[1:])
    volume, upwind, gram, cand_high, cand_low = refs[:5]
    window, mats_high, mats_low, tiles_high, tiles_low = refs[5:10]
    lhs_high, lhs_low, c_high, c_low, same, cross, in_sems, out_sems = refs[10:]

    copies = []
    own = pl.multiple_of(place[0] * 2 * WIDE, 2 * WIDE)
    for piece in range(4):
        if piece == 0:
            sources = [xfactor.at[:, pl.ds(own, WIDE)], xfactor.at[:, pl.ds(own + WIDE, WIDE)]]
        else:
            sources = [mains[piece - 1].at[:, 0:WIDE], mains[piece - 1].at[:, WIDE : 2 * WIDE]]
        if not second:
            sources = [above[piece], sources[0]]
        for side in range(2):
            to = window.at[piece, :, side * WIDE : side * WIDE + WIDE]
            copies.append(pltpu.make_async_copy(sources[side], to, in_sems.at[2 * piece + side]))
    for copy in copies:
        copy.start()

    lane = lax.broadcasted_iota(jnp.int32, (64, 128), 1)
    mats_high[...] = jnp.zeros_like(mats_high)
    mats_low[...] = jnp.zeros_like(mats_low)
    for direc in range(3):
        for side, block in enumerate((volume, upwind)):
            wide = jnp.concatenate([block[direc], block[direc]], axis=1)
            for spot in range(4):
                keep = (lane < 64) if spot % 2 == 0 else (lane >= 64)
                rows = slice(64 * spot, 64 * spot + 64)
                start = 256 * side + 128 * (spot // 2)
                high, low = halves(jnp.where(keep, wide, 0.0))
                mats_high[direc, rows, start : start + 128] = high
                mats_low[direc, rows, start : start + 128] = low
    tiles_high[ZERO_TILE] = jnp.zeros((128, 128), BF16)
    tiles_low[ZERO_TILE] = jnp.zeros((128, 128), BF16)
    for piece in range(4):
        copies[2 * piece].wait()
        copies[2 * piece + 1].wait()
        rows = pl.ds(pl.multiple_of(place[piece] * 32, 32), 32)
        values = window[piece]
        for base, array in ((0, values), (TILES, pltpu.roll(values, 64, 1))):
            for tile in range(TILES):
                high, low = halves(array[:, 128 * tile : 128 * tile + 128])
                tiles_high[base + tile, rows, :] = high
                tiles_low[base + tile, rows, :] = low
    lower = lax.broadcasted_iota(jnp.int32, (128, 128), 1) < 64

    outs = []
    for chunk in range(2):
        for tiles, lhs, cand in ((tiles_high, lhs_high, c_high), (tiles_low, lhs_low, c_low)):
            for pair in range(8):
                tile = tiles[TILES // 2 + chunk * 8 + pair]
                lhs[pair // 2, :, 128 * (pair % 2) : 128 * (pair % 2) + 128] = tile
                lanes = slice(chunk * 1024 + pair * 128, chunk * 1024 + pair * 128 + 128)
                for q in range(4):
                    cand[128 * q : 128 * q + 32, lanes] = tile[32 * q : 32 * q + 32]
        for direc in range(3):
            for pair in range(8):
                one = index[direc, chunk * 16 + 2 * pair]
                two = index[direc, chunk * 16 + 2 * pair + 1]
                at = 256 + 128 * (pair % 2)
                for tiles, lhs in ((tiles_high, lhs_high), (tiles_low, lhs_low)):
                    lhs[pair // 2, :, at : at + 128] = jnp.where(lower, tiles[one], tiles[two])
            high = lhs_high[...].reshape(512, 512)
            low = lhs_low[...].reshape(512, 512)
            moved = product(high, mats_high[direc], (1, 1)) + (
                product(low, mats_high[direc], (1, 1)) + product(high, mats_low[direc], (1, 1))
            )
            parts = halves(moved)
            for group in range(4):
                lanes = slice(chunk * 1024 + group * 256, chunk * 1024 + group * 256 + 256)
                for q in range(4):
                    to = 128 * q + 32 * (direc + 1)
                    rows = slice(128 * group + 32 * q, 128 * group + 32 * q + 32)
                    c_high[to : to + 32, lanes] = parts[0][rows]
                    c_low[to : to + 32, lanes] = parts[1][rows]
        lanes = slice(chunk * 1024, chunk * 1024 + 1024)
        for slot, (held, out) in enumerate(((c_high, cand_high), (c_low, cand_low))):
            sem = out_sems.at[2 * chunk + slot]
            outs.append(pltpu.make_async_copy(held.at[:, lanes], out.at[:, lanes], sem))
            outs[-1].start()
        high, low = c_high[:, lanes], c_low[:, lanes]
        top = product(high[0:256], high, (1, 1))
        bottom = product(high[256:512], high[256:512], (1, 1))
        both = product(high, low, (1, 1))
        if chunk == 0:
            same[0:256, :], same[256:512, 256:512], cross[...] = top, bottom, both
        else:
            same[0:256, :] += top
            same[256:512, 256:512] += bottom
            cross[...] += both

    spot = 0
    for a in range(4):
        for b in range(a, 4):
            rows, cols = slice(128 * a, 128 * a + 128), slice(128 * b, 128 * b + 128)
            total = same[rows, cols] + (cross[rows, cols] + cross[cols, rows].T)
            total = total * (1.0 / 524288)
            to = slice(128 * spot, 128 * spot + 128)
            gram[to, :] = total if second else total + before[to, :]
            spot += 1
    for copy in outs:
        copy.wait()


def transported(second, place, index, xfactor, mains, above, before, volume, upwind):
    part = jax.ShapeDtypeStruct((512, WIDE), BF16)
    extra = [] if second else [*above, before]
    return pl.pallas_call(
        functools.partial(transport_kernel, second),
        out_shape=(jax.ShapeDtypeStruct((1280, 128), F32), part, part),
        in_specs=[SMEM, SMEM, ANY] + [ANY] * 3 + ([] if second else [ANY] * 4 + [VMEM]) + [VMEM, VMEM],
        out_specs=(VMEM, ANY, ANY),
        scratch_shapes=[
            pltpu.VMEM((4, 32, 2 * WIDE), F32),
            pltpu.VMEM((3, 256, 512), BF16),
            pltpu.VMEM((3, 256, 512), BF16),
            pltpu.VMEM((2 * TILES + 1, 128, 128), BF16),
            pltpu.VMEM((2 * TILES + 1, 128, 128), BF16),
            pltpu.VMEM((4, 128, 512), BF16),
            pltpu.VMEM((4, 128, 512), BF16),
            pltpu.VMEM((512, WIDE), BF16),
            pltpu.VMEM((512, WIDE), BF16),
            pltpu.VMEM((512, 512), F32),
            pltpu.VMEM((512, 512), F32),
            pltpu.SemaphoreType.DMA((8,)),
            pltpu.SemaphoreType.DMA((4,)),
        ],
        compiler_params=pltpu.CompilerParams(vmem_limit_bytes=48 << 20),
        cost_estimate=pl.CostEstimate(
            flops=9_000_000_000, bytes_accessed=8 << 20, transcendentals=0
        ),
        name="transport_second" if second else "transport_first",
    )(place, index, xfactor, *mains, *extra, volume, upwind)


def along_lanes(x, lane):
    return jnp.broadcast_to(x[:, lane : lane + 1], (8, 128))


def along_rows(x, row):
    return jnp.broadcast_to(x[row : row + 1, :], (8, 128))


NEAR = 4


def factor_block(left, right):
    row = lax.broadcasted_iota(jnp.int32, (8, 128), 0)
    left, right = list(left), list(right)
    upper, inverse = [], []

    def packed(lines):
        out = lines[0]
        for j in range(1, 8):
            out = jnp.where(row == j, lines[j], out)
        return out

    for step in range(16):
        near = min(16, step + 1 + NEAR)
        c = [[along_lanes(left[i], 8 * step + l) for l in range(8)] for i in range(step, near)]
        s = [[along_rows(c[0][l], i) if i >= l else None for l in range(8)] for i in range(8)]
        lines = [[along_rows(left[step], l) for l in range(8)]]
        lines += [[along_rows(right[step], l) for l in range(8)]]
        lines += c[1:]
        for j in range(8):
            r = lax.rsqrt(s[j][j])
            for i in range(j + 1, 8):
                s[i][j] = s[i][j] * r
            for line in lines:
                line[j] = line[j] * r
            for l in range(j + 1, 8):
                for i in range(l, 8):
                    s[i][l] = s[i][l] - s[i][j] * s[l][j]
                for line in lines:
                    line[l] = line[l] - s[l][j] * line[j]
        wide_left, wide_right, *factors = lines
        upper.append(packed(wide_left))
        inverse.append(packed(wide_right))
        for i in range(step + 1, near):
            for j in range(8):
                left[i] = left[i] - factors[i - step - 1][j] * wide_left[j]
                right[i] = right[i] - factors[i - step - 1][j] * wide_right[j]
        if near < 16:
            both = jnp.concatenate([upper[-1], inverse[-1]], axis=1)
            change = exact(upper[-1][:, 8 * near :], both, (0, 0))
            for i in range(near, 16):
                rows = slice(8 * (i - near), 8 * (i - near) + 8)
                left[i] = left[i] - change[rows, :128]
                right[i] = right[i] - change[rows, 128:]
    return upper, inverse


def factor_kernel(
    place, mine, other, coeffs, high_first, low_first, high_second, low_second, r_out, new_out,
    packed, work, c_high, c_low, held, sems, out_sems,
):
    copies = [
        pltpu.make_async_copy(high_first, c_high.at[:, 0:WIDE], sems.at[0]),
        pltpu.make_async_copy(low_first, c_low.at[:, 0:WIDE], sems.at[1]),
        pltpu.make_async_copy(high_second, c_high.at[:, WIDE : 2 * WIDE], sems.at[2]),
        pltpu.make_async_copy(low_second, c_low.at[:, WIDE : 2 * WIDE], sems.at[3]),
    ]
    for copy in copies:
        copy.start()
    packed[pl.ds(pl.multiple_of(place[0] * 640, 640), 640), :] = mine[...]
    packed[pl.ds(pl.multiple_of((1 - place[0]) * 640, 640), 640), :] = other[...]
    row = lax.broadcasted_iota(jnp.int32, (128, 128), 0)
    col = lax.broadcasted_iota(jnp.int32, (128, 128), 1)
    eye = (row == col).astype(F32)
    zero = jnp.zeros((128, 128), F32)
    at = [slice(128 * a, 128 * a + 128) for a in range(4)]
    beside = [slice(512 + 128 * a, 640 + 128 * a) for a in range(4)]
    spot = 0
    for a in range(4):
        for b in range(4):
            work[at[a], beside[b]] = eye if a == b else zero
            if b >= a:
                work[at[a], at[b]] = packed[128 * spot : 128 * spot + 128, :]
                spot += 1
            else:
                r_out[at[a], at[b]] = zero
    for a in range(4):
        first = 128 * a
        upper, inverse = factor_block(
            [work[first + 8 * i : first + 8 * i + 8, at[a]] for i in range(16)],
            [eye[8 * i : 8 * i + 8] for i in range(16)],
        )
        diag = jnp.where(row >= col, jnp.concatenate(inverse, axis=0), 0.0)
        r_out[at[a], at[a]] = jnp.where(row <= col, jnp.concatenate(upper, axis=0), 0.0)
        work[at[a], beside[a]] = diag
        if a:
            done = slice(512, 512 + first)
            work[at[a], done] = exact(diag, work[at[a], done], (1, 0))
        if a < 3:
            rest = exact(diag, work[at[a], first + 128 : 512], (1, 0))
            r_out[at[a], first + 128 : 512] = rest
            for b in range(a + 1, 4):
                part = rest[:, 128 * (b - a - 1) : 128 * (b - a)]
                right = slice(128 * b, 512)
                work[at[b], right] -= exact(part, rest[:, 128 * (b - a - 1) :], (0, 0))
                done = slice(512, 512 + first + 128)
                work[at[b], done] -= exact(part, work[at[a], done], (0, 0))
    weight_high, weight_low = halves(exact(coeffs[...], work[:, 512:1024], (0, 0)))
    for copy in copies:
        copy.wait()
    outs = []
    for chunk in range(4):
        lanes = slice(chunk * 1024, chunk * 1024 + 1024)
        high, low = c_high[:, lanes], c_low[:, lanes]
        held[:, lanes] = product(weight_high, high, (1, 0)) + (
            product(weight_high, low, (1, 0)) + product(weight_low, high, (1, 0))
        )
        outs.append(pltpu.make_async_copy(held.at[:, lanes], new_out.at[:, lanes], out_sems.at[chunk]))
        outs[-1].start()
    for copy in outs:
        copy.wait()


def factored(place, mine, other, coeffs, parts):
    return pl.pallas_call(
        factor_kernel,
        out_shape=(
            jax.ShapeDtypeStruct((512, 512), F32),
            jax.ShapeDtypeStruct((128, 2 * WIDE), F32),
        ),
        in_specs=[SMEM, VMEM, VMEM, VMEM, ANY, ANY, ANY, ANY],
        out_specs=(VMEM, ANY),
        scratch_shapes=[
            pltpu.VMEM((1280, 128), F32),
            pltpu.VMEM((512, 1024), F32),
            pltpu.VMEM((512, 2 * WIDE), BF16),
            pltpu.VMEM((512, 2 * WIDE), BF16),
            pltpu.VMEM((128, 2 * WIDE), F32),
            pltpu.SemaphoreType.DMA((4,)),
            pltpu.SemaphoreType.DMA((4,)),
        ],
        compiler_params=pltpu.CompilerParams(vmem_limit_bytes=48 << 20),
        name="factor",
    )(place, mine, other, coeffs, *parts)


def sent(value, axis, by):
    count = lax.axis_size(axis)
    return lax.ppermute(value, axis, [(i, (i + by) % count) for i in range(count)])


def pieces_from_here(value, axis):
    count, here = lax.axis_size(axis), lax.axis_index(axis)
    split = value.reshape(count, -1, value.shape[-1])
    return [
        lax.dynamic_index_in_dim(split, (here + by) % count, 0, keepdims=False)
        for by in range(count)
    ]


def scattered_sum(value, axis):
    pieces = pieces_from_here(value, axis)
    return sum((sent(pieces[by], axis, by) for by in range(1, len(pieces))), pieces[0])


def exchanged_sum(value, axis):
    one, two, three = (sent(value, axis, by) for by in range(1, 4))
    return (value + two) + (one + three)


def gathered(value, axis):
    count, here = lax.axis_size(axis), lax.axis_index(axis)
    out = jnp.zeros((count, *value.shape), value.dtype)
    for by in range(count):
        part = sent(value, axis, by) if by else value
        out = lax.dynamic_update_index_in_dim(out, part, (here - by) % count, 0)
    return out.reshape(-1, value.shape[-1])


def summed(gram):
    part = scattered_sum(scattered_sum(gram, "core"), "x")
    part = exchanged_sum(exchanged_sum(part, "y"), "rank")
    mine = gathered(part, "x")
    return mine, sent(mine, "core", 1)


def tile_index(neighbor, first):
    at = neighbor - first
    odd_place = jnp.arange(neighbor.shape[1]) % 2
    tile = jnp.where(at % 2 == odd_place, at // 2, TILES + (at + 1) // 2)
    return jnp.where(neighbor >= 0, tile, ZERO_TILE).astype(jnp.int32)


def shards(xfactor, volume, upwind, neighbor, coeffs):
    sub_elems = neighbor.shape[1] // 4
    rank = lax.axis_index("rank")
    count = lax.axis_size(SPACE)
    above = xfactor[:, 7 * WIDE :]
    above = lax.ppermute(above, SPACE, [(i, i + 1) for i in range(count - 1)])
    mains, halos = [], []
    for by in range(1, 4):
        to = (rank + by) % 4
        piece = lax.dynamic_slice_in_dim(xfactor, to * 2 * WIDE, 2 * WIDE, 1)
        mains.append(sent(piece, "rank", by))
    for by in range(4):
        to = (rank + by) % 4
        inside = lax.dynamic_slice_in_dim(xfactor, jnp.maximum((2 * to - 1) * WIDE, 0), WIDE, 1)
        piece = jnp.where(to == 0, above, inside)
        halos.append(sent(piece, "rank", by) if by else piece)
    place = jnp.stack([(rank - by) % 4 for by in range(4)]).astype(jnp.int32)
    first = (lax.axis_index(SPACE) * 4 + rank) * sub_elems
    own = lax.dynamic_slice_in_dim(neighbor, rank * sub_elems, sub_elems, 1)
    index_first = tile_index(own[:, :HALO_EL], first - HALO_EL)
    index_second = tile_index(own[:, HALO_EL:], first)
    before, *second = transported(
        True, place, index_second, xfactor, mains, None, None, volume, upwind
    )
    gram, *start = transported(
        False, place, index_first, xfactor, mains, halos, before, volume, upwind
    )
    mine, other = summed(gram)
    core = lax.axis_index("core").astype(jnp.int32).reshape(1)
    r_factor, new_factor = factored(core, mine, other, coeffs, [*start, *second])
    return new_factor, r_factor


def solution(mesh):
    finer = Mesh(mesh.devices.reshape(4, 4, 2, 4), SPACE_RANK)
    placed = (P("rank", SPACE), P(), P(), P(None, SPACE), P())
    return jax.shard_map(
        shards, mesh=finer, in_specs=placed, out_specs=(P(None, SPACE_RANK), P()), check_vma=False
    )
```

```python
import functools

import jax
import jax.numpy as jnp
from jax import lax
from jax.experimental import pallas as pl
from jax.experimental.pallas import tpu as pltpu
from jax.sharding import Mesh
from jax.sharding import PartitionSpec as P

SPACE_RANK = ("x", "y", "core", "rank")
SPACE = ("x", "y", "core")
HALO_EL = 32
F32, BF16 = jnp.float32, jnp.bfloat16
VMEM = pl.BlockSpec(memory_space=pltpu.VMEM)
SMEM = pl.BlockSpec(memory_space=pltpu.SMEM)
ANY = pl.BlockSpec(memory_space=pl.ANY)


def halves(x):
    high = x.astype(BF16)
    return high, (x - high.astype(F32)).astype(BF16)


def product(a, b, over):
    dims = (((over[0],), (over[1],)), ((), ()))
    return lax.dot_general(a, b, dims, preferred_element_type=F32)


def exact(a, b, over):
    dims = (((over[0],), (over[1],)), ((), ()))
    return lax.dot_general(
        a, b, dims, precision=lax.Precision.HIGHEST, preferred_element_type=F32
    )


TILES = 32
ZERO_TILE = 2 * TILES
WIDE = 2048


def transport_kernel(second, place, index, xfactor, *refs):
    mains, refs = refs[:3], refs[3:]
    above, refs = ((), refs) if second else (refs[:4], refs[4:])
    before, refs = (None, refs) if second else (refs[0], refs[1:])
    volume, upwind, gram, cand = refs[:4]
    window, mats_high, mats_low, tiles_high, tiles_low = refs[4:9]
    c_high, c_low, same, cross, in_sems, out_sems = refs[9:]

    copies = []
    own = pl.multiple_of(place[0] * 2 * WIDE, 2 * WIDE)
    for piece in range(4):
        if piece == 0:
            sources = [xfactor.at[:, pl.ds(own, WIDE)], xfactor.at[:, pl.ds(own + WIDE, WIDE)]]
        else:
            sources = [mains[piece - 1].at[:, 0:WIDE], mains[piece - 1].at[:, WIDE : 2 * WIDE]]
        if not second:
            sources = [above[piece], sources[0]]
        for side in range(2):
            to = window.at[piece, :, side * WIDE : side * WIDE + WIDE]
            copies.append(pltpu.make_async_copy(sources[side], to, in_sems.at[2 * piece + side]))
    for copy in copies:
        copy.start()

    lane = lax.broadcasted_iota(jnp.int32, (64, 128), 1)
    mats_high[...] = jnp.zeros_like(mats_high)
    mats_low[...] = jnp.zeros_like(mats_low)
    for direc in range(3):
        for side, block in enumerate((volume, upwind)):
            wide = jnp.concatenate([block[direc], block[direc]], axis=1)
            for spot in range(4):
                keep = (lane < 64) if spot % 2 == 0 else (lane >= 64)
                rows = slice(64 * spot, 64 * spot + 64)
                start = 256 * side + 128 * (spot // 2)
                high, low = halves(jnp.where(keep, wide, 0.0))
                mats_high[direc, rows, start : start + 128] = high
                mats_low[direc, rows, start : start + 128] = low
    tiles_high[ZERO_TILE] = jnp.zeros((128, 128), BF16)
    tiles_low[ZERO_TILE] = jnp.zeros((128, 128), BF16)
    for piece in range(4):
        copies[2 * piece].wait()
        copies[2 * piece + 1].wait()
        rows = pl.ds(pl.multiple_of(place[piece] * 32, 32), 32)
        values = window[piece]
        for base, array in ((0, values), (TILES, pltpu.roll(values, 64, 1))):
            for tile in range(TILES):
                high, low = halves(array[:, 128 * tile : 128 * tile + 128])
                tiles_high[base + tile, rows, :] = high
                tiles_low[base + tile, rows, :] = low
    lower = lax.broadcasted_iota(jnp.int32, (128, 128), 1) < 64

    outs = []
    for chunk in range(2):
        for tiles, held in ((tiles_high, c_high), (tiles_low, c_low)):
            for pair in range(8):
                tile = tiles[TILES // 2 + chunk * 8 + pair]
                lanes = slice(chunk * 1024 + pair * 128, chunk * 1024 + pair * 128 + 128)
                for q in range(4):
                    held[128 * q : 128 * q + 32, lanes] = tile[32 * q : 32 * q + 32]
        for direc in range(3):
            high, low = (
                jnp.concatenate(
                    [
                        jnp.concatenate(
                            [tiles[TILES // 2 + chunk * 8 + pair] for pair in (2 * group, 2 * group + 1)]
                            + [
                                jnp.where(
                                    lower,
                                    tiles[index[direc, chunk * 16 + 2 * pair]],
                                    tiles[index[direc, chunk * 16 + 2 * pair + 1]],
                                )
                                for pair in (2 * group, 2 * group + 1)
                            ],
                            axis=1,
                        )
                        for group in range(4)
                    ],
                    axis=0,
                )
                for tiles in (tiles_high, tiles_low)
            )
            moved = product(
                jnp.concatenate([high, low, high], axis=1),
                jnp.concatenate([mats_high[direc], mats_high[direc], mats_low[direc]], axis=1),
                (1, 1),
            )
            parts = halves(moved)
            for group in range(4):
                lanes = slice(chunk * 1024 + group * 256, chunk * 1024 + group * 256 + 256)
                for q in range(4):
                    to = 128 * q + 32 * (direc + 1)
                    rows = slice(128 * group + 32 * q, 128 * group + 32 * q + 32)
                    c_high[to : to + 32, lanes] = parts[0][rows]
                    c_low[to : to + 32, lanes] = parts[1][rows]
        lanes = slice(chunk * 1024, chunk * 1024 + 1024)
        for slot, held in enumerate((c_high, c_low)):
            sem = out_sems.at[2 * chunk + slot]
            outs.append(pltpu.make_async_copy(held.at[:, lanes], cand.at[slot, :, lanes], sem))
            outs[-1].start()
        high, low = c_high[:, lanes], c_low[:, lanes]
        top = product(high[0:256], high, (1, 1))
        bottom = product(high[256:512], high[256:512], (1, 1))
        both = product(high, low, (1, 1))
        if chunk == 0:
            same[0:256, :], same[256:512, 256:512], cross[...] = top, bottom, both
        else:
            same[0:256, :] += top
            same[256:512, 256:512] += bottom
            cross[...] += both

    spot = 0
    for a in range(4):
        for b in range(a, 4):
            rows, cols = slice(128 * a, 128 * a + 128), slice(128 * b, 128 * b + 128)
            total = same[rows, cols] + (cross[rows, cols] + cross[cols, rows].T)
            total = total * (1.0 / 524288)
            to = slice(128 * spot, 128 * spot + 128)
            gram[to, :] = total if second else total + before[to, :]
            spot += 1
    for copy in outs:
        copy.wait()


def transported(second, place, index, xfactor, mains, above, before, volume, upwind):
    part = jax.ShapeDtypeStruct((2, 512, WIDE), BF16)
    extra = [] if second else [*above, before]
    return pl.pallas_call(
        functools.partial(transport_kernel, second),
        out_shape=(jax.ShapeDtypeStruct((1280, 128), F32), part),
        in_specs=[SMEM, SMEM, ANY] + [ANY] * 3 + ([] if second else [ANY] * 4 + [VMEM]) + [VMEM, VMEM],
        out_specs=(VMEM, ANY),
        scratch_shapes=[
            pltpu.VMEM((4, 32, 2 * WIDE), F32),
            pltpu.VMEM((3, 256, 512), BF16),
            pltpu.VMEM((3, 256, 512), BF16),
            pltpu.VMEM((2 * TILES + 1, 128, 128), BF16),
            pltpu.VMEM((2 * TILES + 1, 128, 128), BF16),
            pltpu.VMEM((512, WIDE), BF16),
            pltpu.VMEM((512, WIDE), BF16),
            pltpu.VMEM((512, 512), F32),
            pltpu.VMEM((512, 512), F32),
            pltpu.SemaphoreType.DMA((8,)),
            pltpu.SemaphoreType.DMA((4,)),
        ],
        compiler_params=pltpu.CompilerParams(vmem_limit_bytes=50 << 20),
        cost_estimate=pl.CostEstimate(
            flops=9_000_000_000, bytes_accessed=8 << 20, transcendentals=0
        ),
        name="transport_second" if second else "transport_first",
    )(place, index, xfactor, *mains, *extra, volume, upwind)


def along_lanes(x, lane):
    return jnp.broadcast_to(x[:, lane : lane + 1], (8, 128))


def along_rows(x, row):
    return jnp.broadcast_to(x[row : row + 1, :], (8, 128))


NEAR = 4


def factor_block(left, right):
    row = lax.broadcasted_iota(jnp.int32, (8, 128), 0)
    left, right = list(left), list(right)
    upper, inverse = [], []

    def packed(lines):
        out = lines[0]
        for j in range(1, 8):
            out = jnp.where(row == j, lines[j], out)
        return out

    for step in range(16):
        near = min(16, step + 1 + NEAR)
        c = [[along_lanes(left[i], 8 * step + l) for l in range(8)] for i in range(step, near)]
        s = [[along_rows(c[0][l], i) if i >= l else None for l in range(8)] for i in range(8)]
        lines = [[along_rows(left[step], l) for l in range(8)]]
        lines += [[along_rows(right[step], l) for l in range(8)]]
        lines += c[1:]
        for j in range(8):
            r = lax.rsqrt(s[j][j])
            for i in range(j + 1, 8):
                s[i][j] = s[i][j] * r
            for line in lines:
                line[j] = line[j] * r
            for l in range(j + 1, 8):
                for i in range(l, 8):
                    s[i][l] = s[i][l] - s[i][j] * s[l][j]
                for line in lines:
                    line[l] = line[l] - s[l][j] * line[j]
        wide_left, wide_right, *factors = lines
        upper.append(packed(wide_left))
        inverse.append(packed(wide_right))
        for i in range(step + 1, near):
            for j in range(8):
                left[i] = left[i] - factors[i - step - 1][j] * wide_left[j]
                right[i] = right[i] - factors[i - step - 1][j] * wide_right[j]
        if near < 16:
            both = jnp.concatenate([upper[-1], inverse[-1]], axis=1)
            change = exact(upper[-1][:, 8 * near :], both, (0, 0))
            for i in range(near, 16):
                rows = slice(8 * (i - near), 8 * (i - near) + 8)
                left[i] = left[i] - change[rows, :128]
                right[i] = right[i] - change[rows, 128:]
    return upper, inverse


def factor_kernel(
    place, mine, other, coeffs, cand_first, cand_second, r_out, new_out,
    packed, work, c_high, c_low, new, sems, out_sems,
):
    copies = []
    for side, cand in enumerate((cand_first, cand_second)):
        lanes = slice(side * WIDE, side * WIDE + WIDE)
        for slot, held in enumerate((c_high, c_low)):
            sem = sems.at[2 * side + slot]
            copies.append(pltpu.make_async_copy(cand.at[slot], held.at[:, lanes], sem))
    for copy in copies:
        copy.start()
    packed[pl.ds(pl.multiple_of(place[0] * 640, 640), 640), :] = mine[...]
    packed[pl.ds(pl.multiple_of((1 - place[0]) * 640, 640), 640), :] = other[...]
    row = lax.broadcasted_iota(jnp.int32, (128, 128), 0)
    col = lax.broadcasted_iota(jnp.int32, (128, 128), 1)
    eye = (row == col).astype(F32)
    zero = jnp.zeros((128, 128), F32)
    at = [slice(128 * a, 128 * a + 128) for a in range(4)]
    beside = [slice(512 + 128 * a, 640 + 128 * a) for a in range(4)]
    spot = 0
    for a in range(4):
        for b in range(4):
            work[at[a], beside[b]] = eye if a == b else zero
            if b >= a:
                work[at[a], at[b]] = packed[128 * spot : 128 * spot + 128, :]
                spot += 1
            else:
                r_out[at[a], at[b]] = zero
    for a in range(4):
        first = 128 * a
        upper, inverse = factor_block(
            [work[first + 8 * i : first + 8 * i + 8, at[a]] for i in range(16)],
            [eye[8 * i : 8 * i + 8] for i in range(16)],
        )
        diag = jnp.where(row >= col, jnp.concatenate(inverse, axis=0), 0.0)
        r_out[at[a], at[a]] = jnp.where(row <= col, jnp.concatenate(upper, axis=0), 0.0)
        work[at[a], beside[a]] = diag
        if a:
            done = slice(512, 512 + first)
            work[at[a], done] = exact(diag, work[at[a], done], (1, 0))
        if a < 3:
            rest = exact(diag, work[at[a], first + 128 : 512], (1, 0))
            r_out[at[a], first + 128 : 512] = rest
            for b in range(a + 1, 4):
                part = rest[:, 128 * (b - a - 1) : 128 * (b - a)]
                right = slice(128 * b, 512)
                work[at[b], right] -= exact(part, rest[:, 128 * (b - a - 1) :], (0, 0))
                done = slice(512, 512 + first + 128)
                work[at[b], done] -= exact(part, work[at[a], done], (0, 0))
    weight_high, weight_low = halves(exact(coeffs[...], work[:, 512:1024], (0, 0)))
    for copy in copies:
        copy.wait()
    outs = []
    for chunk in range(4):
        lanes = slice(chunk * 1024, chunk * 1024 + 1024)
        high, low = c_high[:, lanes], c_low[:, lanes]
        new[:, lanes] = product(weight_high, high, (1, 0)) + (
            product(weight_high, low, (1, 0)) + product(weight_low, high, (1, 0))
        )
        outs.append(pltpu.make_async_copy(new.at[:, lanes], new_out.at[:, lanes], out_sems.at[chunk]))
        outs[-1].start()
    for copy in outs:
        copy.wait()


def factored(place, mine, other, coeffs, cand_first, cand_second):
    return pl.pallas_call(
        factor_kernel,
        out_shape=(
            jax.ShapeDtypeStruct((512, 512), F32),
            jax.ShapeDtypeStruct((128, 2 * WIDE), F32),
        ),
        in_specs=[SMEM, VMEM, VMEM, VMEM, ANY, ANY],
        out_specs=(VMEM, ANY),
        scratch_shapes=[
            pltpu.VMEM((1280, 128), F32),
            pltpu.VMEM((512, 1024), F32),
            pltpu.VMEM((512, 2 * WIDE), BF16),
            pltpu.VMEM((512, 2 * WIDE), BF16),
            pltpu.VMEM((128, 2 * WIDE), F32),
            pltpu.SemaphoreType.DMA((4,)),
            pltpu.SemaphoreType.DMA((4,)),
        ],
        compiler_params=pltpu.CompilerParams(vmem_limit_bytes=52 << 20),
        name="factor",
    )(place, mine, other, coeffs, cand_first, cand_second)


def sent(value, axis, by):
    count = lax.axis_size(axis)
    return lax.ppermute(value, axis, [(i, (i + by) % count) for i in range(count)])


def pieces_from_here(value, axis):
    count, here = lax.axis_size(axis), lax.axis_index(axis)
    split = value.reshape(count, -1, value.shape[-1])
    return [
        lax.dynamic_index_in_dim(split, (here + by) % count, 0, keepdims=False)
        for by in range(count)
    ]


def scattered_sum(value, axis):
    pieces = pieces_from_here(value, axis)
    return sum((sent(pieces[by], axis, by) for by in range(1, len(pieces))), pieces[0])


def exchanged_sum(value, axis):
    one, two, three = (sent(value, axis, by) for by in range(1, 4))
    return (value + two) + (one + three)


def gathered(value, axis):
    count, here = lax.axis_size(axis), lax.axis_index(axis)
    out = jnp.zeros((count, *value.shape), value.dtype)
    for by in range(count):
        part = sent(value, axis, by) if by else value
        out = lax.dynamic_update_index_in_dim(out, part, (here - by) % count, 0)
    return out.reshape(-1, value.shape[-1])


def summed(gram):
    part = scattered_sum(scattered_sum(gram, "core"), "x")
    part = exchanged_sum(exchanged_sum(part, "y"), "rank")
    mine = gathered(part, "x")
    return mine, sent(mine, "core", 1)


def tile_index(neighbor, first):
    at = neighbor - first
    odd_place = jnp.arange(neighbor.shape[1]) % 2
    tile = jnp.where(at % 2 == odd_place, at // 2, TILES + (at + 1) // 2)
    return jnp.where(neighbor >= 0, tile, ZERO_TILE).astype(jnp.int32)


def shards(xfactor, volume, upwind, neighbor, coeffs):
    sub_elems = neighbor.shape[1] // 4
    rank = lax.axis_index("rank")
    count = lax.axis_size(SPACE)
    above = xfactor[:, 7 * WIDE :]
    above = lax.ppermute(above, SPACE, [(i, i + 1) for i in range(count - 1)])
    mains, halos = [], []
    for by in range(1, 4):
        to = (rank + by) % 4
        piece = lax.dynamic_slice_in_dim(xfactor, to * 2 * WIDE, 2 * WIDE, 1)
        mains.append(sent(piece, "rank", by))
    for by in range(4):
        to = (rank + by) % 4
        inside = lax.dynamic_slice_in_dim(xfactor, jnp.maximum((2 * to - 1) * WIDE, 0), WIDE, 1)
        piece = jnp.where(to == 0, above, inside)
        halos.append(sent(piece, "rank", by) if by else piece)
    place = jnp.stack([(rank - by) % 4 for by in range(4)]).astype(jnp.int32)
    first = (lax.axis_index(SPACE) * 4 + rank) * sub_elems
    own = lax.dynamic_slice_in_dim(neighbor, rank * sub_elems, sub_elems, 1)
    index_first = tile_index(own[:, :HALO_EL], first - HALO_EL)
    index_second = tile_index(own[:, HALO_EL:], first)
    before, second = transported(
        True, place, index_second, xfactor, mains, None, None, volume, upwind
    )
    gram, start = transported(
        False, place, index_first, xfactor, mains, halos, before, volume, upwind
    )
    mine, other = summed(gram)
    core = lax.axis_index("core").astype(jnp.int32).reshape(1)
    r_factor, new_factor = factored(core, mine, other, coeffs, start, second)
    return new_factor, r_factor


def solution(mesh):
    finer = Mesh(mesh.devices.reshape(4, 4, 2, 4), SPACE_RANK)
    placed = (P("rank", SPACE), P(), P(), P(None, SPACE), P())
    return jax.shard_map(
        shards, mesh=finer, in_specs=placed, out_specs=(P(None, SPACE_RANK), P()), check_vma=False
    )
```

```python
import functools

import jax
import jax.numpy as jnp
from jax import lax
from jax.experimental import pallas as pl
from jax.experimental.pallas import tpu as pltpu
from jax.sharding import Mesh
from jax.sharding import PartitionSpec as P

SPACE_RANK = ("x", "y", "core", "rank")
SPACE = ("x", "y", "core")
HALO_EL = 32
F32, BF16 = jnp.float32, jnp.bfloat16
VMEM = pl.BlockSpec(memory_space=pltpu.VMEM)
SMEM = pl.BlockSpec(memory_space=pltpu.SMEM)
ANY = pl.BlockSpec(memory_space=pl.ANY)


def halves(x):
    high = x.astype(BF16)
    return high, (x - high.astype(F32)).astype(BF16)


def product(a, b, over):
    dims = (((over[0],), (over[1],)), ((), ()))
    return lax.dot_general(a, b, dims, preferred_element_type=F32)


def exact(a, b, over):
    dims = (((over[0],), (over[1],)), ((), ()))
    return lax.dot_general(
        a, b, dims, precision=lax.Precision.HIGHEST, preferred_element_type=F32
    )


TILES = 32
ZERO_TILE = 2 * TILES
WIDE = 2048


def transport_kernel(second, place, index, xfactor, *refs):
    mains, refs = refs[:3], refs[3:]
    above, refs = ((), refs) if second else (refs[:4], refs[4:])
    before, refs = (None, refs) if second else (refs[0], refs[1:])
    volume, upwind, *refs = refs
    grams, refs = (refs[:1], refs[1:]) if second else (refs[:2], refs[2:])
    cand, window, mats_high, mats_low, tiles_high, tiles_low = refs[:6]
    c_high, c_low, same, cross, packed, added, in_sems, out_sems = refs[6:]

    copies = []
    own = pl.multiple_of(place[0] * 2 * WIDE, 2 * WIDE)
    for piece in range(4):
        if piece == 0:
            sources = [xfactor.at[:, pl.ds(own, WIDE)], xfactor.at[:, pl.ds(own + WIDE, WIDE)]]
        else:
            sources = [mains[piece - 1].at[:, 0:WIDE], mains[piece - 1].at[:, WIDE : 2 * WIDE]]
        if not second:
            sources = [above[piece], sources[0]]
        for side in range(2):
            to = window.at[piece, :, side * WIDE : side * WIDE + WIDE]
            copies.append(pltpu.make_async_copy(sources[side], to, in_sems.at[2 * piece + side]))
    if not second:
        copies.append(pltpu.make_async_copy(before, added, in_sems.at[8]))
    for copy in copies:
        copy.start()

    lane = lax.broadcasted_iota(jnp.int32, (64, 128), 1)
    mats_high[...] = jnp.zeros_like(mats_high)
    mats_low[...] = jnp.zeros_like(mats_low)
    for direc in range(3):
        for side, block in enumerate((volume, upwind)):
            wide = jnp.concatenate([block[direc], block[direc]], axis=1)
            for spot in range(4):
                keep = (lane < 64) if spot % 2 == 0 else (lane >= 64)
                rows = slice(64 * spot, 64 * spot + 64)
                start = 256 * side + 128 * (spot // 2)
                high, low = halves(jnp.where(keep, wide, 0.0))
                mats_high[direc, rows, start : start + 128] = high
                mats_low[direc, rows, start : start + 128] = low
    tiles_high[ZERO_TILE] = jnp.zeros((128, 128), BF16)
    tiles_low[ZERO_TILE] = jnp.zeros((128, 128), BF16)
    for piece in range(4):
        copies[2 * piece].wait()
        copies[2 * piece + 1].wait()
        rows = pl.ds(pl.multiple_of(place[piece] * 32, 32), 32)
        values = window[piece]
        for base, array in ((0, values), (TILES, pltpu.roll(values, 64, 1))):
            for tile in range(TILES):
                high, low = halves(array[:, 128 * tile : 128 * tile + 128])
                tiles_high[base + tile, rows, :] = high
                tiles_low[base + tile, rows, :] = low
    lower = lax.broadcasted_iota(jnp.int32, (128, 128), 1) < 64

    outs = []
    for chunk in range(2):
        for tiles, held in ((tiles_high, c_high), (tiles_low, c_low)):
            for pair in range(8):
                tile = tiles[TILES // 2 + chunk * 8 + pair]
                lanes = slice(chunk * 1024 + pair * 128, chunk * 1024 + pair * 128 + 128)
                for q in range(4):
                    held[128 * q : 128 * q + 32, lanes] = tile[32 * q : 32 * q + 32]
        for direc in range(3):
            high, low = (
                jnp.concatenate(
                    [
                        jnp.concatenate(
                            [tiles[TILES // 2 + chunk * 8 + pair] for pair in (2 * group, 2 * group + 1)]
                            + [
                                jnp.where(
                                    lower,
                                    tiles[index[direc, chunk * 16 + 2 * pair]],
                                    tiles[index[direc, chunk * 16 + 2 * pair + 1]],
                                )
                                for pair in (2 * group, 2 * group + 1)
                            ],
                            axis=1,
                        )
                        for group in range(4)
                    ],
                    axis=0,
                )
                for tiles in (tiles_high, tiles_low)
            )
            moved = product(
                jnp.concatenate([high, low, high], axis=1),
                jnp.concatenate([mats_high[direc], mats_high[direc], mats_low[direc]], axis=1),
                (1, 1),
            )
            parts = halves(moved)
            for group in range(4):
                lanes = slice(chunk * 1024 + group * 256, chunk * 1024 + group * 256 + 256)
                for q in range(4):
                    to = 128 * q + 32 * (direc + 1)
                    rows = slice(128 * group + 32 * q, 128 * group + 32 * q + 32)
                    c_high[to : to + 32, lanes] = parts[0][rows]
                    c_low[to : to + 32, lanes] = parts[1][rows]
        lanes = slice(chunk * 1024, chunk * 1024 + 1024)
        for slot, held in enumerate((c_high, c_low)):
            sem = out_sems.at[2 * chunk + slot]
            outs.append(pltpu.make_async_copy(held.at[:, lanes], cand.at[slot, :, lanes], sem))
            outs[-1].start()
        high, low = c_high[:, lanes], c_low[:, lanes]
        top = product(high[0:256], high, (1, 1))
        bottom = product(high[256:512], high[256:512], (1, 1))
        both = product(high, low, (1, 1))
        if chunk == 0:
            same[0:256, :], same[256:512, 256:512], cross[...] = top, bottom, both
        else:
            same[0:256, :] += top
            same[256:512, 256:512] += bottom
            cross[...] += both

    if not second:
        copies[8].wait()
    spot = 0
    for a in range(4):
        for b in range(a, 4):
            rows, cols = slice(128 * a, 128 * a + 128), slice(128 * b, 128 * b + 128)
            total = same[rows, cols] + (cross[rows, cols] + cross[cols, rows].T)
            total = total * (1.0 / 524288)
            to = slice(128 * spot, 128 * spot + 128)
            packed[to, :] = total if second else total + added[to, :]
            spot += 1
    if second:
        outs.append(pltpu.make_async_copy(packed, grams[0], out_sems.at[4]))
        outs[-1].start()
    else:
        for half in range(2):
            core = place[4] if half == 0 else 1 - place[4]
            grams[half][...] = packed[pl.ds(pl.multiple_of(core * 640, 640), 640), :]
    for copy in outs:
        copy.wait()


def transported(second, place, index, xfactor, mains, above, before, volume, upwind):
    part = jax.ShapeDtypeStruct((2, 512, WIDE), BF16)
    extra = [] if second else [*above, before]
    shapes = [(1280, 128)] if second else [(640, 128), (640, 128)]
    grams = [jax.ShapeDtypeStruct(shape, F32) for shape in shapes]
    return pl.pallas_call(
        functools.partial(transport_kernel, second),
        out_shape=(*grams, part),
        in_specs=[SMEM, SMEM, ANY] + [ANY] * 3 + ([] if second else [ANY] * 5) + [VMEM, VMEM],
        out_specs=(ANY, ANY) if second else (VMEM, VMEM, ANY),
        scratch_shapes=[
            pltpu.VMEM((4, 32, 2 * WIDE), F32),
            pltpu.VMEM((3, 256, 512), BF16),
            pltpu.VMEM((3, 256, 512), BF16),
            pltpu.VMEM((2 * TILES + 1, 128, 128), BF16),
            pltpu.VMEM((2 * TILES + 1, 128, 128), BF16),
            pltpu.VMEM((512, WIDE), BF16),
            pltpu.VMEM((512, WIDE), BF16),
            pltpu.VMEM((512, 512), F32),
            pltpu.VMEM((512, 512), F32),
            pltpu.VMEM((1280, 128), F32),
            pltpu.VMEM((1280, 128), F32),
            pltpu.SemaphoreType.DMA((9,)),
            pltpu.SemaphoreType.DMA((5,)),
        ],
        compiler_params=pltpu.CompilerParams(vmem_limit_bytes=50 << 20),
        cost_estimate=pl.CostEstimate(
            flops=9_000_000_000, bytes_accessed=8 << 20, transcendentals=0
        ),
        name="transport_second" if second else "transport_first",
    )(place, index, xfactor, *mains, *extra, volume, upwind)


def along_lanes(x, lane):
    return jnp.broadcast_to(x[:, lane : lane + 1], (8, 128))


def along_rows(x, row):
    return jnp.broadcast_to(x[row : row + 1, :], (8, 128))


def tree_sum(terms):
    while len(terms) > 1:
        terms = [sum(terms[i : i + 2][1:], terms[i]) for i in range(0, len(terms), 2)]
    return terms[0]


NEAR = 5


def factor_block(left, right, spread):
    row = lax.broadcasted_iota(jnp.int32, (8, 128), 0)
    left, right = list(left), list(right)
    upper, inverse = [], []

    def packed(lines):
        out = lines[0]
        for j in range(1, 8):
            out = jnp.where(row == j, lines[j], out)
        return out

    for step in range(16):
        near = min(16, step + 1 + NEAR)
        c = [[along_lanes(left[i], 8 * step + l) for l in range(8)] for i in range(step, near)]
        for l in range(8):
            spread[8 * step + l] = c[0][l]
        s = [
            [along_rows(spread[8 * step + l, i : i + 1, :], 0) if i >= l else None for l in range(8)]
            for i in range(8)
        ]
        lines = [[along_rows(left[step], l) for l in range(8)]]
        lines += [[along_rows(right[step], l) for l in range(8)]]
        lines += c[1:]
        for j in range(8):
            r = lax.rsqrt(s[j][j])
            for i in range(j + 1, 8):
                s[i][j] = s[i][j] * r
            for line in lines:
                line[j] = line[j] * r
            for l in range(j + 1, 8):
                for i in range(l, 8):
                    s[i][l] = s[i][l] - s[i][j] * s[l][j]
                for line in lines:
                    line[l] = line[l] - s[l][j] * line[j]
        wide_left, wide_right, *factors = lines
        upper.append(packed(wide_left))
        inverse.append(packed(wide_right))
        for i in range(step + 1, near):
            left[i] = left[i] - tree_sum([a * b for a, b in zip(factors[i - step - 1], wide_left)])
            right[i] = right[i] - tree_sum([a * b for a, b in zip(factors[i - step - 1], wide_right)])
        if near < 16:
            both = jnp.concatenate([upper[-1], inverse[-1]], axis=1)
            change = exact(upper[-1][:, 8 * near :], both, (0, 0))
            for i in range(near, 16):
                rows = slice(8 * (i - near), 8 * (i - near) + 8)
                left[i] = left[i] - change[rows, :128]
                right[i] = right[i] - change[rows, 128:]
    return upper, inverse


def factor_kernel(
    place, mine, other, coeffs, cand_first, cand_second, r_out, new_out,
    packed, work, spread, r_held, c_high, c_low, new, sems, out_sems,
):
    copies = []
    for side, cand in enumerate((cand_first, cand_second)):
        lanes = slice(side * WIDE, side * WIDE + WIDE)
        for slot, held in enumerate((c_high, c_low)):
            sem = sems.at[2 * side + slot]
            copies.append(pltpu.make_async_copy(cand.at[slot], held.at[:, lanes], sem))
    for copy in copies:
        copy.start()
    packed[pl.ds(pl.multiple_of(place[0] * 640, 640), 640), :] = mine[...]
    packed[pl.ds(pl.multiple_of((1 - place[0]) * 640, 640), 640), :] = other[...]
    row = lax.broadcasted_iota(jnp.int32, (128, 128), 0)
    col = lax.broadcasted_iota(jnp.int32, (128, 128), 1)
    eye = (row == col).astype(F32)
    zero = jnp.zeros((128, 128), F32)
    at = [slice(128 * a, 128 * a + 128) for a in range(4)]
    beside = [slice(512 + 128 * a, 640 + 128 * a) for a in range(4)]
    spot = 0
    for a in range(4):
        for b in range(4):
            work[at[a], beside[b]] = eye if a == b else zero
            if b >= a:
                work[at[a], at[b]] = packed[128 * spot : 128 * spot + 128, :]
                spot += 1
            else:
                r_held[at[a], at[b]] = zero
    for a in range(4):
        first = 128 * a
        upper, inverse = factor_block(
            [work[first + 8 * i : first + 8 * i + 8, at[a]] for i in range(16)],
            [eye[8 * i : 8 * i + 8] for i in range(16)],
            spread.at[a],
        )
        diag = jnp.where(row >= col, jnp.concatenate(inverse, axis=0), 0.0)
        r_held[at[a], at[a]] = jnp.where(row <= col, jnp.concatenate(upper, axis=0), 0.0)
        work[at[a], beside[a]] = diag
        if a:
            done = slice(512, 512 + first)
            work[at[a], done] = exact(diag, work[at[a], done], (1, 0))
        if a < 3:
            rest = exact(diag, work[at[a], first + 128 : 512], (1, 0))
            r_held[at[a], first + 128 : 512] = rest
            for b in range(a + 1, 4):
                part = rest[:, 128 * (b - a - 1) : 128 * (b - a)]
                right = slice(128 * b, 512)
                work[at[b], right] -= exact(part, rest[:, 128 * (b - a - 1) :], (0, 0))
                done = slice(512, 512 + first + 128)
                work[at[b], done] -= exact(part, work[at[a], done], (0, 0))
    outs = [pltpu.make_async_copy(r_held, r_out, out_sems.at[4])]
    outs[0].start()
    weight_high, weight_low = halves(exact(coeffs[...], work[:, 512:1024], (0, 0)))
    weights = jnp.concatenate([weight_high, weight_low], axis=0)
    for copy in copies:
        copy.wait()
    for chunk in range(4):
        lanes = slice(chunk * 1024, chunk * 1024 + 1024)
        both = product(weights, c_high[:, lanes], (1, 0))
        low = product(weight_high, c_low[:, lanes], (1, 0))
        new[:, lanes] = both[0:128] + (both[128:256] + low)
        outs.append(pltpu.make_async_copy(new.at[:, lanes], new_out.at[:, lanes], out_sems.at[chunk]))
        outs[-1].start()
    for copy in outs:
        copy.wait()


def factored(place, mine, other, coeffs, cand_first, cand_second):
    return pl.pallas_call(
        factor_kernel,
        out_shape=(
            jax.ShapeDtypeStruct((512, 512), F32),
            jax.ShapeDtypeStruct((128, 2 * WIDE), F32),
        ),
        in_specs=[SMEM, VMEM, VMEM, VMEM, ANY, ANY],
        out_specs=(ANY, ANY),
        scratch_shapes=[
            pltpu.VMEM((1280, 128), F32),
            pltpu.VMEM((512, 1024), F32),
            pltpu.VMEM((4, 128, 8, 128), F32),
            pltpu.VMEM((512, 512), F32),
            pltpu.VMEM((512, 2 * WIDE), BF16),
            pltpu.VMEM((512, 2 * WIDE), BF16),
            pltpu.VMEM((128, 2 * WIDE), F32),
            pltpu.SemaphoreType.DMA((4,)),
            pltpu.SemaphoreType.DMA((5,)),
        ],
        compiler_params=pltpu.CompilerParams(vmem_limit_bytes=52 << 20),
        name="factor",
    )(place, mine, other, coeffs, cand_first, cand_second)


def sent(value, axis, by):
    count = lax.axis_size(axis)
    return lax.ppermute(value, axis, [(i, (i + by) % count) for i in range(count)])


def pieces_from_here(value, axis):
    count, here = lax.axis_size(axis), lax.axis_index(axis)
    split = value.reshape(count, -1, value.shape[-1])
    return [
        lax.dynamic_index_in_dim(split, (here + by) % count, 0, keepdims=False)
        for by in range(count)
    ]


def scattered_sum(value, axis):
    pieces = pieces_from_here(value, axis)
    return sum((sent(pieces[by], axis, by) for by in range(1, len(pieces))), pieces[0])


def exchanged_sum(value, axis):
    one, two, three = (sent(value, axis, by) for by in range(1, 4))
    return (value + two) + (one + three)


def gathered(value, axis):
    count, here = lax.axis_size(axis), lax.axis_index(axis)
    out = jnp.zeros((count, *value.shape), value.dtype)
    for by in range(count):
        part = sent(value, axis, by) if by else value
        out = lax.dynamic_update_index_in_dim(out, part, (here - by) % count, 0)
    return out.reshape(-1, value.shape[-1])


def summed(keep, send):
    part = scattered_sum(keep + sent(send, "core", 1), "x")
    part = exchanged_sum(exchanged_sum(part, "y"), "rank")
    mine = gathered(part, "x")
    return mine, sent(mine, "core", 1)


def tile_index(neighbor, first):
    at = neighbor - first
    odd_place = jnp.arange(neighbor.shape[1]) % 2
    tile = jnp.where(at % 2 == odd_place, at // 2, TILES + (at + 1) // 2)
    return jnp.where(neighbor >= 0, tile, ZERO_TILE).astype(jnp.int32)


def shards(xfactor, volume, upwind, neighbor, coeffs):
    sub_elems = neighbor.shape[1] // 4
    rank = lax.axis_index("rank")
    count = lax.axis_size(SPACE)
    above = xfactor[:, 7 * WIDE :]
    above = lax.ppermute(above, SPACE, [(i, i + 1) for i in range(count - 1)])
    mains, halos = [], []
    for by in range(1, 4):
        to = (rank + by) % 4
        piece = lax.dynamic_slice_in_dim(xfactor, to * 2 * WIDE, 2 * WIDE, 1)
        mains.append(sent(piece, "rank", by))
    for by in range(4):
        to = (rank + by) % 4
        inside = lax.dynamic_slice_in_dim(xfactor, jnp.maximum((2 * to - 1) * WIDE, 0), WIDE, 1)
        piece = jnp.where(to == 0, above, inside)
        halos.append(sent(piece, "rank", by) if by else piece)
    core = lax.axis_index("core")
    place = jnp.stack([(rank - by) % 4 for by in range(4)] + [core]).astype(jnp.int32)
    first = (lax.axis_index(SPACE) * 4 + rank) * sub_elems
    own = lax.dynamic_slice_in_dim(neighbor, rank * sub_elems, sub_elems, 1)
    index_first = tile_index(own[:, :HALO_EL], first - HALO_EL)
    index_second = tile_index(own[:, HALO_EL:], first)
    before, second = transported(
        True, place, index_second, xfactor, mains, None, None, volume, upwind
    )
    keep, send, start = transported(
        False, place, index_first, xfactor, mains, halos, before, volume, upwind
    )
    mine, other = summed(keep, send)
    r_factor, new_factor = factored(place[4:], mine, other, coeffs, start, second)
    return new_factor, r_factor


def solution(mesh):
    finer = Mesh(mesh.devices.reshape(4, 4, 2, 4), SPACE_RANK)
    placed = (P("rank", SPACE), P(), P(), P(None, SPACE), P())
    return jax.shard_map(
        shards, mesh=finer, in_specs=placed, out_specs=(P(None, SPACE_RANK), P()), check_vma=False
    )
```

```python
import functools

import jax
import jax.numpy as jnp
from jax import lax
from jax.experimental import pallas as pl
from jax.experimental.pallas import tpu as pltpu
from jax.sharding import Mesh
from jax.sharding import PartitionSpec as P

SPACE_RANK = ("x", "y", "core", "rank")
SPACE = ("x", "y", "core")
HALO_EL = 32
F32, BF16 = jnp.float32, jnp.bfloat16
VMEM = pl.BlockSpec(memory_space=pltpu.VMEM)
SMEM = pl.BlockSpec(memory_space=pltpu.SMEM)
ANY = pl.BlockSpec(memory_space=pl.ANY)


def halves(x):
    high = x.astype(BF16)
    return high, (x - high.astype(F32)).astype(BF16)


def product(a, b, over):
    dims = (((over[0],), (over[1],)), ((), ()))
    return lax.dot_general(a, b, dims, preferred_element_type=F32)


def exact(a, b, over):
    dims = (((over[0],), (over[1],)), ((), ()))
    return lax.dot_general(
        a, b, dims, precision=lax.Precision.HIGHEST, preferred_element_type=F32
    )


TILES = 32
ZERO_TILE = 2 * TILES
WIDE = 2048


def transport_kernel(second, place, index, xfactor, *refs):
    mains, refs = refs[:3], refs[3:]
    above, refs = ((), refs) if second else (refs[:4], refs[4:])
    before, refs = (None, refs) if second else (refs[0], refs[1:])
    volume, upwind, *refs = refs
    grams, refs = (refs[:1], refs[1:]) if second else (refs[:2], refs[2:])
    cand, window, mats_high, mats_low, tiles_high, tiles_low = refs[:6]
    c_high, c_low, same, cross, packed, added, in_sems, out_sems = refs[6:]

    copies = []
    own = pl.multiple_of(place[0] * 2 * WIDE, 2 * WIDE)
    for piece in range(4):
        if piece == 0:
            sources = [xfactor.at[:, pl.ds(own, WIDE)], xfactor.at[:, pl.ds(own + WIDE, WIDE)]]
        else:
            sources = [mains[piece - 1].at[:, 0:WIDE], mains[piece - 1].at[:, WIDE : 2 * WIDE]]
        if not second:
            sources = [above[piece], sources[0]]
        for side in range(2):
            to = window.at[piece, :, side * WIDE : side * WIDE + WIDE]
            copies.append(pltpu.make_async_copy(sources[side], to, in_sems.at[2 * piece + side]))
    if not second:
        copies.append(pltpu.make_async_copy(before.at[0:1280, :], added, in_sems.at[8]))
    for copy in copies:
        copy.start()

    lane = lax.broadcasted_iota(jnp.int32, (64, 128), 1)
    mats_high[...] = jnp.zeros_like(mats_high)
    mats_low[...] = jnp.zeros_like(mats_low)
    for direc in range(3):
        for side, block in enumerate((volume, upwind)):
            wide = jnp.concatenate([block[direc], block[direc]], axis=1)
            for spot in range(4):
                keep = (lane < 64) if spot % 2 == 0 else (lane >= 64)
                rows = slice(64 * spot, 64 * spot + 64)
                start = 256 * side + 128 * (spot // 2)
                high, low = halves(jnp.where(keep, wide, 0.0))
                mats_high[direc, rows, start : start + 128] = high
                mats_low[direc, rows, start : start + 128] = low
    tiles_high[ZERO_TILE] = jnp.zeros((128, 128), BF16)
    tiles_low[ZERO_TILE] = jnp.zeros((128, 128), BF16)
    for piece in range(4):
        copies[2 * piece].wait()
        copies[2 * piece + 1].wait()
        rows = pl.ds(pl.multiple_of(place[piece] * 32, 32), 32)
        values = window[piece]
        for base, array in ((0, values), (TILES, pltpu.roll(values, 64, 1))):
            for tile in range(TILES):
                high, low = halves(array[:, 128 * tile : 128 * tile + 128])
                tiles_high[base + tile, rows, :] = high
                tiles_low[base + tile, rows, :] = low
    lower = lax.broadcasted_iota(jnp.int32, (128, 128), 1) < 64

    outs = []
    for chunk in range(2):
        for tiles, held in ((tiles_high, c_high), (tiles_low, c_low)):
            for pair in range(8):
                tile = tiles[TILES // 2 + chunk * 8 + pair]
                lanes = slice(chunk * 1024 + pair * 128, chunk * 1024 + pair * 128 + 128)
                for q in range(4):
                    held[128 * q : 128 * q + 32, lanes] = tile[32 * q : 32 * q + 32]
        for direc in range(3):
            high, low = (
                jnp.concatenate(
                    [
                        jnp.concatenate(
                            [tiles[TILES // 2 + chunk * 8 + pair] for pair in (2 * group, 2 * group + 1)]
                            + [
                                jnp.where(
                                    lower,
                                    tiles[index[direc, chunk * 16 + 2 * pair]],
                                    tiles[index[direc, chunk * 16 + 2 * pair + 1]],
                                )
                                for pair in (2 * group, 2 * group + 1)
                            ],
                            axis=1,
                        )
                        for group in range(4)
                    ],
                    axis=0,
                )
                for tiles in (tiles_high, tiles_low)
            )
            moved = product(
                jnp.concatenate([high, low, high], axis=1),
                jnp.concatenate([mats_high[direc], mats_high[direc], mats_low[direc]], axis=1),
                (1, 1),
            )
            parts = halves(moved)
            for group in range(4):
                lanes = slice(chunk * 1024 + group * 256, chunk * 1024 + group * 256 + 256)
                for q in range(4):
                    to = 128 * q + 32 * (direc + 1)
                    rows = slice(128 * group + 32 * q, 128 * group + 32 * q + 32)
                    c_high[to : to + 32, lanes] = parts[0][rows]
                    c_low[to : to + 32, lanes] = parts[1][rows]
        lanes = slice(chunk * 1024, chunk * 1024 + 1024)
        for slot, held in enumerate((c_high, c_low)):
            sem = out_sems.at[2 * chunk + slot]
            outs.append(pltpu.make_async_copy(held.at[:, lanes], cand.at[slot, :, lanes], sem))
            outs[-1].start()
        high, low = c_high[:, lanes], c_low[:, lanes]
        top = product(high[0:256], high, (1, 1))
        bottom = product(high[256:512], high[256:512], (1, 1))
        both = product(high, low, (1, 1))
        if chunk == 0:
            same[0:256, :], same[256:512, 256:512], cross[...] = top, bottom, both
        else:
            same[0:256, :] += top
            same[256:512, 256:512] += bottom
            cross[...] += both

    if not second:
        copies[8].wait()
    spot = 0
    for a in range(4):
        for b in range(a, 4):
            rows, cols = slice(128 * a, 128 * a + 128), slice(128 * b, 128 * b + 128)
            total = same[rows, cols] + (cross[rows, cols] + cross[cols, rows].T)
            total = total * (1.0 / 524288)
            to = slice(128 * spot, 128 * spot + 128)
            packed[to, :] = total if second else total + added[to, :]
            spot += 1
    if second:
        outs.append(pltpu.make_async_copy(packed, grams[0].at[0:1280, :], out_sems.at[4]))
        outs[-1].start()
    else:
        for half in range(2):
            core = place[4] if half == 0 else 1 - place[4]
            grams[half][...] = packed[pl.ds(pl.multiple_of(core * 640, 640), 640), :]
    for copy in outs:
        copy.wait()


def transported(second, place, index, xfactor, mains, above, before, volume, upwind):
    part = jax.ShapeDtypeStruct((2, 512, WIDE), BF16)
    extra = [] if second else [*above, before]
    shapes = [(1280, 128)] if second else [(640, 128), (640, 128)]
    grams = [jax.ShapeDtypeStruct(shape, F32) for shape in shapes]
    return pl.pallas_call(
        functools.partial(transport_kernel, second),
        out_shape=(*grams, part),
        in_specs=[SMEM, SMEM, ANY] + [ANY] * 3 + ([] if second else [ANY] * 5) + [VMEM, VMEM],
        out_specs=(ANY, ANY) if second else (VMEM, VMEM, ANY),
        scratch_shapes=[
            pltpu.VMEM((4, 32, 2 * WIDE), F32),
            pltpu.VMEM((3, 256, 512), BF16),
            pltpu.VMEM((3, 256, 512), BF16),
            pltpu.VMEM((2 * TILES + 1, 128, 128), BF16),
            pltpu.VMEM((2 * TILES + 1, 128, 128), BF16),
            pltpu.VMEM((512, WIDE), BF16),
            pltpu.VMEM((512, WIDE), BF16),
            pltpu.VMEM((512, 512), F32),
            pltpu.VMEM((512, 512), F32),
            pltpu.VMEM((1280, 128), F32),
            pltpu.VMEM((1280, 128), F32),
            pltpu.SemaphoreType.DMA((9,)),
            pltpu.SemaphoreType.DMA((5,)),
        ],
        compiler_params=pltpu.CompilerParams(vmem_limit_bytes=50 << 20),
        cost_estimate=pl.CostEstimate(
            flops=9_000_000_000, bytes_accessed=8 << 20, transcendentals=0
        ),
        name="transport_second" if second else "transport_first",
    )(place, index, xfactor, *mains, *extra, volume, upwind)


def along_lanes(x, lane):
    return jnp.broadcast_to(x[:, lane : lane + 1], (8, 128))


def along_rows(x, row):
    return jnp.broadcast_to(x[row : row + 1, :], (8, 128))


def tree_sum(terms):
    while len(terms) > 1:
        terms = [sum(terms[i : i + 2][1:], terms[i]) for i in range(0, len(terms), 2)]
    return terms[0]


NEAR = 5


def factor_block(left, right, spread):
    row = lax.broadcasted_iota(jnp.int32, (8, 128), 0)
    left, right = list(left), list(right)
    upper, inverse = [], []

    def packed(lines):
        out = lines[0]
        for j in range(1, 8):
            out = jnp.where(row == j, lines[j], out)
        return out

    for step in range(16):
        near = min(16, step + 1 + NEAR)
        c = [[along_lanes(left[i], 8 * step + l) for l in range(8)] for i in range(step, near)]
        for l in range(8):
            spread[8 * step + l] = c[0][l]
        s = [
            [along_rows(spread[8 * step + l, i : i + 1, :], 0) if i >= l else None for l in range(8)]
            for i in range(8)
        ]
        lines = [[along_rows(left[step], l) for l in range(8)]]
        lines += [[along_rows(right[step], l) for l in range(8)]]
        lines += c[1:]
        for j in range(8):
            r = lax.rsqrt(s[j][j])
            for i in range(j + 1, 8):
                s[i][j] = s[i][j] * r
            for line in lines:
                line[j] = line[j] * r
            for l in range(j + 1, 8):
                for i in range(l, 8):
                    s[i][l] = s[i][l] - s[i][j] * s[l][j]
                for line in lines:
                    line[l] = line[l] - s[l][j] * line[j]
        wide_left, wide_right, *factors = lines
        upper.append(packed(wide_left))
        inverse.append(packed(wide_right))
        for i in range(step + 1, near):
            left[i] = left[i] - tree_sum([a * b for a, b in zip(factors[i - step - 1], wide_left)])
            right[i] = right[i] - tree_sum([a * b for a, b in zip(factors[i - step - 1], wide_right)])
        if near < 16:
            both = jnp.concatenate([upper[-1], inverse[-1]], axis=1)
            change = exact(upper[-1][:, 8 * near :], both, (0, 0))
            for i in range(near, 16):
                rows = slice(8 * (i - near), 8 * (i - near) + 8)
                left[i] = left[i] - change[rows, :128]
                right[i] = right[i] - change[rows, 128:]
    return upper, inverse


def factor_kernel(
    place, mine, other, coeffs, cand_first, cand_second, r_out, new_out,
    packed, work, spread, r_held, c_high, c_low, new, sems, out_sems,
):
    copies = []
    for side, cand in enumerate((cand_first, cand_second)):
        lanes = slice(side * WIDE, side * WIDE + WIDE)
        for slot, held in enumerate((c_high, c_low)):
            sem = sems.at[2 * side + slot]
            copies.append(pltpu.make_async_copy(cand.at[slot], held.at[:, lanes], sem))
    for copy in copies:
        copy.start()
    packed[pl.ds(pl.multiple_of(place[0] * 640, 640), 640), :] = mine[...]
    packed[pl.ds(pl.multiple_of((1 - place[0]) * 640, 640), 640), :] = other[...]
    row = lax.broadcasted_iota(jnp.int32, (128, 128), 0)
    col = lax.broadcasted_iota(jnp.int32, (128, 128), 1)
    eye = (row == col).astype(F32)
    zero = jnp.zeros((128, 128), F32)
    at = [slice(128 * a, 128 * a + 128) for a in range(4)]
    beside = [slice(512 + 128 * a, 640 + 128 * a) for a in range(4)]
    spot = 0
    for a in range(4):
        for b in range(4):
            work[at[a], beside[b]] = eye if a == b else zero
            if b >= a:
                work[at[a], at[b]] = packed[128 * spot : 128 * spot + 128, :]
                spot += 1
            else:
                r_held[at[a], at[b]] = zero
    for a in range(4):
        first = 128 * a
        upper, inverse = factor_block(
            [work[first + 8 * i : first + 8 * i + 8, at[a]] for i in range(16)],
            [eye[8 * i : 8 * i + 8] for i in range(16)],
            spread.at[a],
        )
        diag = jnp.where(row >= col, jnp.concatenate(inverse, axis=0), 0.0)
        r_held[at[a], at[a]] = jnp.where(row <= col, jnp.concatenate(upper, axis=0), 0.0)
        work[at[a], beside[a]] = diag
        if a:
            done = slice(512, 512 + first)
            work[at[a], done] = exact(diag, work[at[a], done], (1, 0))
        if a < 3:
            rest = exact(diag, work[at[a], first + 128 : 512], (1, 0))
            r_held[at[a], first + 128 : 512] = rest
            for b in range(a + 1, 4):
                part = rest[:, 128 * (b - a - 1) : 128 * (b - a)]
                right = slice(128 * b, 512)
                work[at[b], right] -= exact(part, rest[:, 128 * (b - a - 1) :], (0, 0))
                done = slice(512, 512 + first + 128)
                work[at[b], done] -= exact(part, work[at[a], done], (0, 0))
    outs = [pltpu.make_async_copy(r_held, r_out, out_sems.at[4])]
    outs[0].start()
    weight_high, weight_low = halves(exact(coeffs[...], work[:, 512:1024], (0, 0)))
    weights = jnp.concatenate([weight_high, weight_low], axis=0)
    for copy in copies:
        copy.wait()
    for chunk in range(4):
        lanes = slice(chunk * 1024, chunk * 1024 + 1024)
        both = product(weights, c_high[:, lanes], (1, 0))
        low = product(weight_high, c_low[:, lanes], (1, 0))
        new[:, lanes] = both[0:128] + (both[128:256] + low)
        outs.append(pltpu.make_async_copy(new.at[:, lanes], new_out.at[:, lanes], out_sems.at[chunk]))
        outs[-1].start()
    for copy in outs:
        copy.wait()


def factored(place, mine, other, coeffs, cand_first, cand_second):
    return pl.pallas_call(
        factor_kernel,
        out_shape=(
            jax.ShapeDtypeStruct((512, 512), F32),
            jax.ShapeDtypeStruct((128, 2 * WIDE), F32),
        ),
        in_specs=[SMEM, VMEM, VMEM, VMEM, ANY, ANY],
        out_specs=(ANY, ANY),
        scratch_shapes=[
            pltpu.VMEM((1280, 128), F32),
            pltpu.VMEM((512, 1024), F32),
            pltpu.VMEM((4, 128, 8, 128), F32),
            pltpu.VMEM((512, 512), F32),
            pltpu.VMEM((512, 2 * WIDE), BF16),
            pltpu.VMEM((512, 2 * WIDE), BF16),
            pltpu.VMEM((128, 2 * WIDE), F32),
            pltpu.SemaphoreType.DMA((4,)),
            pltpu.SemaphoreType.DMA((5,)),
        ],
        compiler_params=pltpu.CompilerParams(vmem_limit_bytes=52 << 20),
        name="factor",
    )(place, mine, other, coeffs, cand_first, cand_second)


def sent(value, axis, by):
    count = lax.axis_size(axis)
    return lax.ppermute(value, axis, [(i, (i + by) % count) for i in range(count)])


def pieces_from_here(value, axis):
    count, here = lax.axis_size(axis), lax.axis_index(axis)
    split = value.reshape(count, -1, value.shape[-1])
    return [
        lax.dynamic_index_in_dim(split, (here + by) % count, 0, keepdims=False)
        for by in range(count)
    ]


def scattered_sum(value, axis):
    pieces = pieces_from_here(value, axis)
    return sum((sent(pieces[by], axis, by) for by in range(1, len(pieces))), pieces[0])


def exchanged_sum(value, axis):
    one, two, three = (sent(value, axis, by) for by in range(1, 4))
    return (value + two) + (one + three)


def gathered(value, axis):
    count, here = lax.axis_size(axis), lax.axis_index(axis)
    out = jnp.zeros((count, *value.shape), value.dtype)
    for by in range(count):
        part = sent(value, axis, by) if by else value
        out = lax.dynamic_update_index_in_dim(out, part, (here - by) % count, 0)
    return out.reshape(-1, value.shape[-1])


def summed(keep, send):
    part = scattered_sum(keep + sent(send, "core", 1), "x")
    part = exchanged_sum(exchanged_sum(part, "y"), "rank")
    mine = gathered(part, "x")
    return mine, sent(mine, "core", 1)


def tile_index(neighbor, first):
    at = neighbor - first
    odd_place = jnp.arange(neighbor.shape[1]) % 2
    tile = jnp.where(at % 2 == odd_place, at // 2, TILES + (at + 1) // 2)
    return jnp.where(neighbor >= 0, tile, ZERO_TILE).astype(jnp.int32)


def shards(xfactor, volume, upwind, neighbor, coeffs):
    sub_elems = neighbor.shape[1] // 4
    rank = lax.axis_index("rank")
    count = lax.axis_size(SPACE)
    above = xfactor[:, 7 * WIDE :]
    above = lax.ppermute(above, SPACE, [(i, i + 1) for i in range(count - 1)])
    order = (2, 1, 3)
    mains, halos = [], []
    for by in order:
        to = (rank + by) % 4
        piece = lax.dynamic_slice_in_dim(xfactor, to * 2 * WIDE, 2 * WIDE, 1)
        mains.append(sent(piece, "rank", by))
    for by in (0, *order):
        to = (rank + by) % 4
        inside = lax.dynamic_slice_in_dim(xfactor, jnp.maximum((2 * to - 1) * WIDE, 0), WIDE, 1)
        piece = jnp.where(to == 0, above, inside)
        halos.append(sent(piece, "rank", by) if by else piece)
    core = lax.axis_index("core")
    place = jnp.stack([(rank - by) % 4 for by in (0, *order)] + [core]).astype(jnp.int32)
    first = (lax.axis_index(SPACE) * 4 + rank) * sub_elems
    own = lax.dynamic_slice_in_dim(neighbor, rank * sub_elems, sub_elems, 1)
    index_first = tile_index(own[:, :HALO_EL], first - HALO_EL)
    index_second = tile_index(own[:, HALO_EL:], first)
    before, second = transported(
        True, place, index_second, xfactor, mains, None, None, volume, upwind
    )
    keep, send, start = transported(
        False, place, index_first, xfactor, mains, halos, before, volume, upwind
    )
    mine, other = summed(keep, send)
    r_factor, new_factor = factored(place[4:], mine, other, coeffs, start, second)
    return new_factor, r_factor


def solution(mesh):
    finer = Mesh(mesh.devices.reshape(4, 4, 2, 4), SPACE_RANK)
    placed = (P("rank", SPACE), P(), P(), P(None, SPACE), P())
    return jax.shard_map(
        shards, mesh=finer, in_specs=placed, out_specs=(P(None, SPACE_RANK), P()), check_vma=False
    )
```

```python
import functools

import jax
import jax.numpy as jnp
from jax import lax
from jax.experimental import pallas as pl
from jax.experimental.pallas import tpu as pltpu
from jax.sharding import Mesh
from jax.sharding import PartitionSpec as P

SPACE_RANK = ("x", "y", "core", "rank")
SPACE = ("x", "y", "core")
HALO_EL = 32
F32, BF16 = jnp.float32, jnp.bfloat16
VMEM = pl.BlockSpec(memory_space=pltpu.VMEM)
SMEM = pl.BlockSpec(memory_space=pltpu.SMEM)
ANY = pl.BlockSpec(memory_space=pl.ANY)


def halves(x):
    high = x.astype(BF16)
    return high, (x - high.astype(F32)).astype(BF16)


def product(a, b, over):
    dims = (((over[0],), (over[1],)), ((), ()))
    return lax.dot_general(a, b, dims, preferred_element_type=F32)


def exact(a, b, over):
    dims = (((over[0],), (over[1],)), ((), ()))
    return lax.dot_general(
        a, b, dims, precision=lax.Precision.HIGHEST, preferred_element_type=F32
    )


TILES = 32
ZERO_TILE = 2 * TILES
WIDE = 2048


def transport_kernel(second, place, index, xfactor, *refs):
    mains, refs = refs[:3], refs[3:]
    above, refs = ((), refs) if second else (refs[:4], refs[4:])
    before, refs = (None, refs) if second else (refs[0], refs[1:])
    volume, upwind, *refs = refs
    grams, refs = (refs[:1], refs[1:]) if second else (refs[:2], refs[2:])
    cand, window, mats_high, mats_low, tiles_high, tiles_low = refs[:6]
    c_high, c_low, same, cross, packed, added, in_sems, out_sems = refs[6:]

    copies = []
    own = pl.multiple_of(place[0] * 2 * WIDE, 2 * WIDE)
    for piece in range(4):
        if piece == 0:
            sources = [xfactor.at[:, pl.ds(own, WIDE)], xfactor.at[:, pl.ds(own + WIDE, WIDE)]]
        else:
            sources = [mains[piece - 1].at[:, 0:WIDE], mains[piece - 1].at[:, WIDE : 2 * WIDE]]
        if not second:
            sources = [above[piece], sources[0]]
        for side in range(2):
            to = window.at[piece, :, side * WIDE : side * WIDE + WIDE]
            copies.append(pltpu.make_async_copy(sources[side], to, in_sems.at[2 * piece + side]))
    if not second:
        copies.append(pltpu.make_async_copy(before.at[0:1280, :], added, in_sems.at[8]))
    for copy in copies:
        copy.start()

    lane = lax.broadcasted_iota(jnp.int32, (64, 128), 1)
    mats_high[...] = jnp.zeros_like(mats_high)
    mats_low[...] = jnp.zeros_like(mats_low)
    for direc in range(3):
        for side, block in enumerate((volume, upwind)):
            wide = jnp.concatenate([block[direc], block[direc]], axis=1)
            for spot in range(4):
                keep = (lane < 64) if spot % 2 == 0 else (lane >= 64)
                rows = slice(64 * spot, 64 * spot + 64)
                start = 256 * side + 128 * (spot // 2)
                high, low = halves(jnp.where(keep, wide, 0.0))
                mats_high[direc, rows, start : start + 128] = high
                mats_low[direc, rows, start : start + 128] = low
    tiles_high[ZERO_TILE] = jnp.zeros((128, 128), BF16)
    tiles_low[ZERO_TILE] = jnp.zeros((128, 128), BF16)
    for piece in range(4):
        copies[2 * piece].wait()
        copies[2 * piece + 1].wait()
        rows = pl.ds(pl.multiple_of(place[piece] * 32, 32), 32)
        values = window[piece]
        for base, array in ((0, values), (TILES, pltpu.roll(values, 64, 1))):
            for tile in range(TILES):
                high, low = halves(array[:, 128 * tile : 128 * tile + 128])
                tiles_high[base + tile, rows, :] = high
                tiles_low[base + tile, rows, :] = low
    lower = lax.broadcasted_iota(jnp.int32, (128, 128), 1) < 64

    outs = []
    for chunk in range(2):
        for tiles, held in ((tiles_high, c_high), (tiles_low, c_low)):
            for pair in range(8):
                tile = tiles[TILES // 2 + chunk * 8 + pair]
                lanes = slice(chunk * 1024 + pair * 128, chunk * 1024 + pair * 128 + 128)
                for q in range(4):
                    held[128 * q : 128 * q + 32, lanes] = tile[32 * q : 32 * q + 32]
        for direc in range(3):
            high, low = (
                jnp.concatenate(
                    [
                        jnp.concatenate(
                            [tiles[TILES // 2 + chunk * 8 + pair] for pair in (2 * group, 2 * group + 1)]
                            + [
                                jnp.where(
                                    lower,
                                    tiles[index[direc, chunk * 16 + 2 * pair]],
                                    tiles[index[direc, chunk * 16 + 2 * pair + 1]],
                                )
                                for pair in (2 * group, 2 * group + 1)
                            ],
                            axis=1,
                        )
                        for group in range(4)
                    ],
                    axis=0,
                )
                for tiles in (tiles_high, tiles_low)
            )
            moved = product(
                jnp.concatenate([high, low, high], axis=1),
                jnp.concatenate([mats_high[direc], mats_high[direc], mats_low[direc]], axis=1),
                (1, 1),
            )
            parts = halves(moved)
            for group in range(4):
                lanes = slice(chunk * 1024 + group * 256, chunk * 1024 + group * 256 + 256)
                for q in range(4):
                    to = 128 * q + 32 * (direc + 1)
                    rows = slice(128 * group + 32 * q, 128 * group + 32 * q + 32)
                    c_high[to : to + 32, lanes] = parts[0][rows]
                    c_low[to : to + 32, lanes] = parts[1][rows]
        lanes = slice(chunk * 1024, chunk * 1024 + 1024)
        for slot, held in enumerate((c_high, c_low)):
            sem = out_sems.at[2 * chunk + slot]
            outs.append(pltpu.make_async_copy(held.at[:, lanes], cand.at[slot, :, lanes], sem))
            outs[-1].start()
        high, low = c_high[:, lanes], c_low[:, lanes]
        top = product(high[0:256], high, (1, 1))
        bottom = product(high[256:512], high[256:512], (1, 1))
        both = product(high, low, (1, 1))
        if chunk == 0:
            same[0:256, :], same[256:512, 256:512], cross[...] = top, bottom, both
        else:
            same[0:256, :] += top
            same[256:512, 256:512] += bottom
            cross[...] += both

    if not second:
        copies[8].wait()
    spot = 0
    for a in range(4):
        for b in range(a, 4):
            rows, cols = slice(128 * a, 128 * a + 128), slice(128 * b, 128 * b + 128)
            total = same[rows, cols] + (cross[rows, cols] + cross[cols, rows].T)
            total = total * (1.0 / 524288)
            to = slice(128 * spot, 128 * spot + 128)
            packed[to, :] = total if second else total + added[to, :]
            spot += 1
    if second:
        outs.append(pltpu.make_async_copy(packed, grams[0].at[0:1280, :], out_sems.at[4]))
        outs[-1].start()
    else:
        for half in range(2):
            core = place[4] if half == 0 else 1 - place[4]
            grams[half][...] = packed[pl.ds(pl.multiple_of(core * 640, 640), 640), :]
    for copy in outs:
        copy.wait()


def transported(second, place, index, xfactor, mains, above, before, volume, upwind):
    part = jax.ShapeDtypeStruct((2, 512, WIDE), BF16)
    extra = [] if second else [*above, before]
    shapes = [(1280, 128)] if second else [(640, 128), (640, 128)]
    grams = [jax.ShapeDtypeStruct(shape, F32) for shape in shapes]
    return pl.pallas_call(
        functools.partial(transport_kernel, second),
        out_shape=(*grams, part),
        in_specs=[SMEM, SMEM, ANY] + [ANY] * 3 + ([] if second else [ANY] * 5) + [VMEM, VMEM],
        out_specs=(ANY, ANY) if second else (VMEM, VMEM, ANY),
        scratch_shapes=[
            pltpu.VMEM((4, 32, 2 * WIDE), F32),
            pltpu.VMEM((3, 256, 512), BF16),
            pltpu.VMEM((3, 256, 512), BF16),
            pltpu.VMEM((2 * TILES + 1, 128, 128), BF16),
            pltpu.VMEM((2 * TILES + 1, 128, 128), BF16),
            pltpu.VMEM((512, WIDE), BF16),
            pltpu.VMEM((512, WIDE), BF16),
            pltpu.VMEM((512, 512), F32),
            pltpu.VMEM((512, 512), F32),
            pltpu.VMEM((1280, 128), F32),
            pltpu.VMEM((1280, 128), F32),
            pltpu.SemaphoreType.DMA((9,)),
            pltpu.SemaphoreType.DMA((5,)),
        ],
        compiler_params=pltpu.CompilerParams(vmem_limit_bytes=50 << 20),
        cost_estimate=pl.CostEstimate(
            flops=9_000_000_000, bytes_accessed=8 << 20, transcendentals=0
        ),
        name="transport_second" if second else "transport_first",
    )(place, index, xfactor, *mains, *extra, volume, upwind)


def along_lanes(x, lane):
    return jnp.broadcast_to(x[:, lane : lane + 1], (8, 128))


def along_rows(x, row):
    return jnp.broadcast_to(x[row : row + 1, :], (8, 128))


def tree_sum(terms):
    while len(terms) > 1:
        terms = [sum(terms[i : i + 2][1:], terms[i]) for i in range(0, len(terms), 2)]
    return terms[0]


NEAR = 5


def factor_block(left, right, spread):
    row = lax.broadcasted_iota(jnp.int32, (8, 128), 0)
    left, right = list(left), list(right)
    upper, inverse = [], []

    def packed(lines):
        out = lines[0]
        for j in range(1, 8):
            out = jnp.where(row == j, lines[j], out)
        return out

    for step in range(16):
        near = min(16, step + 1 + NEAR)
        c = [[along_lanes(left[i], 8 * step + l) for l in range(8)] for i in range(step, near)]
        for l in range(8):
            spread[8 * step + l] = c[0][l]
        s = [
            [along_rows(spread[8 * step + l, i : i + 1, :], 0) if i >= l else None for l in range(8)]
            for i in range(8)
        ]
        lines = [[along_rows(left[step], l) for l in range(8)]]
        lines += [[along_rows(right[step], l) for l in range(8)]]
        lines += c[1:]
        for j in range(8):
            r = lax.rsqrt(s[j][j])
            for i in range(j + 1, 8):
                s[i][j] = s[i][j] * r
            for line in lines:
                line[j] = line[j] * r
            for l in range(j + 1, 8):
                for i in range(l, 8):
                    s[i][l] = s[i][l] - s[i][j] * s[l][j]
                for line in lines:
                    line[l] = line[l] - s[l][j] * line[j]
        wide_left, wide_right, *factors = lines
        upper.append(packed(wide_left))
        inverse.append(packed(wide_right))
        for i in range(step + 1, near):
            left[i] = left[i] - tree_sum([a * b for a, b in zip(factors[i - step - 1], wide_left)])
            right[i] = right[i] - tree_sum([a * b for a, b in zip(factors[i - step - 1], wide_right)])
        if near < 16:
            both = jnp.concatenate([upper[-1], inverse[-1]], axis=1)
            change = exact(upper[-1][:, 8 * near :], both, (0, 0))
            for i in range(near, 16):
                rows = slice(8 * (i - near), 8 * (i - near) + 8)
                left[i] = left[i] - change[rows, :128]
                right[i] = right[i] - change[rows, 128:]
    return upper, inverse


def factor_kernel(
    place, mine, other, coeffs, cand_first, cand_second, r_out, new_out,
    packed, work, spread, r_held, c_high, c_low, new, sems, out_sems,
):
    copies = []
    for side, cand in enumerate((cand_first, cand_second)):
        lanes = slice(side * WIDE, side * WIDE + WIDE)
        for slot, held in enumerate((c_high, c_low)):
            sem = sems.at[2 * side + slot]
            copies.append(pltpu.make_async_copy(cand.at[slot], held.at[:, lanes], sem))
    for copy in copies:
        copy.start()
    packed[pl.ds(pl.multiple_of(place[0] * 640, 640), 640), :] = mine[...]
    packed[pl.ds(pl.multiple_of((1 - place[0]) * 640, 640), 640), :] = other[...]
    row = lax.broadcasted_iota(jnp.int32, (128, 128), 0)
    col = lax.broadcasted_iota(jnp.int32, (128, 128), 1)
    eye = (row == col).astype(F32)
    zero = jnp.zeros((128, 128), F32)
    at = [slice(128 * a, 128 * a + 128) for a in range(4)]
    beside = [slice(512 + 128 * a, 640 + 128 * a) for a in range(4)]
    spot = 0
    for a in range(4):
        for b in range(4):
            work[at[a], beside[b]] = eye if a == b else zero
            if b >= a:
                work[at[a], at[b]] = packed[128 * spot : 128 * spot + 128, :]
                spot += 1
            else:
                r_held[at[a], at[b]] = zero
    for a in range(4):
        first = 128 * a
        upper, inverse = factor_block(
            [work[first + 8 * i : first + 8 * i + 8, at[a]] for i in range(16)],
            [eye[8 * i : 8 * i + 8] for i in range(16)],
            spread.at[a],
        )
        diag = jnp.where(row >= col, jnp.concatenate(inverse, axis=0), 0.0)
        r_held[at[a], at[a]] = jnp.where(row <= col, jnp.concatenate(upper, axis=0), 0.0)
        work[at[a], beside[a]] = diag
        if a:
            done = slice(512, 512 + first)
            work[at[a], done] = exact(diag, work[at[a], done], (1, 0))
        if a < 3:
            rest = exact(diag, work[at[a], first + 128 : 512], (1, 0))
            r_held[at[a], first + 128 : 512] = rest
            for b in range(a + 1, 4):
                part = rest[:, 128 * (b - a - 1) : 128 * (b - a)]
                right = slice(128 * b, 512)
                work[at[b], right] -= exact(part, rest[:, 128 * (b - a - 1) :], (0, 0))
                done = slice(512, 512 + first + 128)
                work[at[b], done] -= exact(part, work[at[a], done], (0, 0))
    outs = [pltpu.make_async_copy(r_held, r_out, out_sems.at[4])]
    outs[0].start()
    weight_high, weight_low = halves(exact(coeffs[...], work[:, 512:1024], (0, 0)))
    weights = jnp.concatenate([weight_high, weight_low], axis=0)
    for copy in copies:
        copy.wait()
    for chunk in range(4):
        lanes = slice(chunk * 1024, chunk * 1024 + 1024)
        both = product(weights, c_high[:, lanes], (1, 0))
        low = product(weight_high, c_low[:, lanes], (1, 0))
        new[:, lanes] = both[0:128] + (both[128:256] + low)
        outs.append(pltpu.make_async_copy(new.at[:, lanes], new_out.at[:, lanes], out_sems.at[chunk]))
        outs[-1].start()
    for copy in outs:
        copy.wait()


def factored(place, mine, other, coeffs, cand_first, cand_second):
    return pl.pallas_call(
        factor_kernel,
        out_shape=(
            jax.ShapeDtypeStruct((512, 512), F32),
            jax.ShapeDtypeStruct((128, 2 * WIDE), F32),
        ),
        in_specs=[SMEM, VMEM, VMEM, VMEM, ANY, ANY],
        out_specs=(ANY, ANY),
        scratch_shapes=[
            pltpu.VMEM((1280, 128), F32),
            pltpu.VMEM((512, 1024), F32),
            pltpu.VMEM((4, 128, 8, 128), F32),
            pltpu.VMEM((512, 512), F32),
            pltpu.VMEM((512, 2 * WIDE), BF16),
            pltpu.VMEM((512, 2 * WIDE), BF16),
            pltpu.VMEM((128, 2 * WIDE), F32),
            pltpu.SemaphoreType.DMA((4,)),
            pltpu.SemaphoreType.DMA((5,)),
        ],
        compiler_params=pltpu.CompilerParams(vmem_limit_bytes=52 << 20),
        name="factor",
    )(place, mine, other, coeffs, cand_first, cand_second)


def sent(value, axis, by):
    count = lax.axis_size(axis)
    return lax.ppermute(value, axis, [(i, (i + by) % count) for i in range(count)])


def pieces_from_here(value, axis):
    count, here = lax.axis_size(axis), lax.axis_index(axis)
    split = value.reshape(count, -1, value.shape[-1])
    return [
        lax.dynamic_index_in_dim(split, (here + by) % count, 0, keepdims=False)
        for by in range(count)
    ]


def scattered_sum(value, axis):
    pieces = pieces_from_here(value, axis)
    two, one, three = (sent(pieces[by], axis, by) for by in (2, 1, 3))
    return (pieces[0] + two) + (one + three)


def exchanged_sum(value, axis):
    one, two, three = (sent(value, axis, by) for by in range(1, 4))
    return (value + two) + (one + three)


def gathered(value, axis):
    count, here = lax.axis_size(axis), lax.axis_index(axis)
    out = jnp.zeros((count, *value.shape), value.dtype)
    for by in (0, 2, 1, 3):
        part = sent(value, axis, by) if by else value
        out = lax.dynamic_update_index_in_dim(out, part, (here - by) % count, 0)
    return out.reshape(-1, value.shape[-1])


def summed(keep, send):
    part = scattered_sum(keep + sent(send, "core", 1), "x")
    part = exchanged_sum(exchanged_sum(part, "y"), "rank")
    mine = gathered(part, "x")
    return mine, sent(mine, "core", 1)


def tile_index(neighbor, first):
    at = neighbor - first
    odd_place = jnp.arange(neighbor.shape[1]) % 2
    tile = jnp.where(at % 2 == odd_place, at // 2, TILES + (at + 1) // 2)
    return jnp.where(neighbor >= 0, tile, ZERO_TILE).astype(jnp.int32)


def shards(xfactor, volume, upwind, neighbor, coeffs):
    sub_elems = neighbor.shape[1] // 4
    rank = lax.axis_index("rank")
    count = lax.axis_size(SPACE)
    above = xfactor[:, 7 * WIDE :]
    above = lax.ppermute(above, SPACE, [(i, i + 1) for i in range(count - 1)])
    order = (2, 1, 3)
    mains, halos = [], []
    for by in order:
        to = (rank + by) % 4
        piece = lax.dynamic_slice_in_dim(xfactor, to * 2 * WIDE, 2 * WIDE, 1)
        mains.append(sent(piece, "rank", by))
    for by in (0, *order):
        to = (rank + by) % 4
        inside = lax.dynamic_slice_in_dim(xfactor, jnp.maximum((2 * to - 1) * WIDE, 0), WIDE, 1)
        piece = jnp.where(to == 0, above, inside)
        halos.append(sent(piece, "rank", by) if by else piece)
    core = lax.axis_index("core")
    place = jnp.stack([(rank - by) % 4 for by in (0, *order)] + [core]).astype(jnp.int32)
    first = (lax.axis_index(SPACE) * 4 + rank) * sub_elems
    own = lax.dynamic_slice_in_dim(neighbor, rank * sub_elems, sub_elems, 1)
    index_first = tile_index(own[:, :HALO_EL], first - HALO_EL)
    index_second = tile_index(own[:, HALO_EL:], first)
    before, second = transported(
        True, place, index_second, xfactor, mains, None, None, volume, upwind
    )
    keep, send, start = transported(
        False, place, index_first, xfactor, mains, halos, before, volume, upwind
    )
    mine, other = summed(keep, send)
    r_factor, new_factor = factored(place[4:], mine, other, coeffs, start, second)
    return new_factor, r_factor


def solution(mesh):
    finer = Mesh(mesh.devices.reshape(4, 4, 2, 4), SPACE_RANK)
    placed = (P("rank", SPACE), P(), P(), P(None, SPACE), P())
    return jax.shard_map(
        shards, mesh=finer, in_specs=placed, out_specs=(P(None, SPACE_RANK), P()), check_vma=False
    )
```

```python
import functools

import jax
import jax.numpy as jnp
from jax import lax
from jax.experimental import pallas as pl
from jax.experimental.pallas import tpu as pltpu
from jax.sharding import Mesh
from jax.sharding import PartitionSpec as P

SPACE_RANK = ("x", "y", "core", "rank")
SPACE = ("x", "y", "core")
HALO_EL = 32
F32, BF16 = jnp.float32, jnp.bfloat16
VMEM = pl.BlockSpec(memory_space=pltpu.VMEM)
SMEM = pl.BlockSpec(memory_space=pltpu.SMEM)
ANY = pl.BlockSpec(memory_space=pl.ANY)


def halves(x):
    high = x.astype(BF16)
    return high, (x - high.astype(F32)).astype(BF16)


def product(a, b, over):
    dims = (((over[0],), (over[1],)), ((), ()))
    return lax.dot_general(a, b, dims, preferred_element_type=F32)


def exact(a, b, over):
    dims = (((over[0],), (over[1],)), ((), ()))
    return lax.dot_general(
        a, b, dims, precision=lax.Precision.HIGHEST, preferred_element_type=F32
    )


TILES = 32
ZERO_TILE = 2 * TILES
WIDE = 2048


def transport_kernel(second, place, index, xfactor, *refs):
    mains, refs = refs[:3], refs[3:]
    above, refs = ((), refs) if second else (refs[:4], refs[4:])
    before, refs = (None, refs) if second else (refs[0], refs[1:])
    volume, upwind, *refs = refs
    grams, refs = (refs[:1], refs[1:]) if second else (refs[:2], refs[2:])
    cand, window, mats_high, mats_low, tiles_high, tiles_low = refs[:6]
    c_high, c_low, same, cross, packed, added, in_sems, out_sems = refs[6:]

    copies = []
    own = pl.multiple_of(place[0] * 2 * WIDE, 2 * WIDE)
    for piece in range(4):
        if piece == 0:
            sources = [xfactor.at[:, pl.ds(own, WIDE)], xfactor.at[:, pl.ds(own + WIDE, WIDE)]]
        else:
            sources = [mains[piece - 1].at[:, 0:WIDE], mains[piece - 1].at[:, WIDE : 2 * WIDE]]
        if not second:
            sources = [above[piece], sources[0]]
        for side in range(2):
            to = window.at[piece, :, side * WIDE : side * WIDE + WIDE]
            copies.append(pltpu.make_async_copy(sources[side], to, in_sems.at[2 * piece + side]))
    if not second:
        copies.append(pltpu.make_async_copy(before.at[0:1280, :], added, in_sems.at[8]))
    for copy in copies:
        copy.start()

    lane = lax.broadcasted_iota(jnp.int32, (64, 128), 1)
    mats_high[...] = jnp.zeros_like(mats_high)
    mats_low[...] = jnp.zeros_like(mats_low)
    for direc in range(3):
        for side, block in enumerate((volume, upwind)):
            wide = jnp.concatenate([block[direc], block[direc]], axis=1)
            for spot in range(4):
                keep = (lane < 64) if spot % 2 == 0 else (lane >= 64)
                rows = slice(64 * spot, 64 * spot + 64)
                start = 256 * side + 128 * (spot // 2)
                high, low = halves(jnp.where(keep, wide, 0.0))
                mats_high[direc, rows, start : start + 128] = high
                mats_low[direc, rows, start : start + 128] = low
    tiles_high[ZERO_TILE] = jnp.zeros((128, 128), BF16)
    tiles_low[ZERO_TILE] = jnp.zeros((128, 128), BF16)
    for piece in range(4):
        copies[2 * piece].wait()
        copies[2 * piece + 1].wait()
        rows = pl.ds(pl.multiple_of(place[piece] * 32, 32), 32)
        values = window[piece]
        for base, array in ((0, values), (TILES, pltpu.roll(values, 64, 1))):
            for tile in range(TILES):
                high, low = halves(array[:, 128 * tile : 128 * tile + 128])
                tiles_high[base + tile, rows, :] = high
                tiles_low[base + tile, rows, :] = low
    lower = lax.broadcasted_iota(jnp.int32, (128, 128), 1) < 64

    outs = []
    for chunk in range(2):
        for tiles, held in ((tiles_high, c_high), (tiles_low, c_low)):
            for pair in range(8):
                tile = tiles[TILES // 2 + chunk * 8 + pair]
                lanes = slice(chunk * 1024 + pair * 128, chunk * 1024 + pair * 128 + 128)
                for q in range(4):
                    held[128 * q : 128 * q + 32, lanes] = tile[32 * q : 32 * q + 32]
        for direc in range(3):
            high, low = (
                jnp.concatenate(
                    [
                        jnp.concatenate(
                            [tiles[TILES // 2 + chunk * 8 + pair] for pair in (2 * group, 2 * group + 1)]
                            + [
                                jnp.where(
                                    lower,
                                    tiles[index[direc, chunk * 16 + 2 * pair]],
                                    tiles[index[direc, chunk * 16 + 2 * pair + 1]],
                                )
                                for pair in (2 * group, 2 * group + 1)
                            ],
                            axis=1,
                        )
                        for group in range(4)
                    ],
                    axis=0,
                )
                for tiles in (tiles_high, tiles_low)
            )
            moved = product(
                jnp.concatenate([high, low, high], axis=1),
                jnp.concatenate([mats_high[direc], mats_high[direc], mats_low[direc]], axis=1),
                (1, 1),
            )
            parts = halves(moved)
            for group in range(4):
                lanes = slice(chunk * 1024 + group * 256, chunk * 1024 + group * 256 + 256)
                for q in range(4):
                    to = 128 * q + 32 * (direc + 1)
                    rows = slice(128 * group + 32 * q, 128 * group + 32 * q + 32)
                    c_high[to : to + 32, lanes] = parts[0][rows]
                    c_low[to : to + 32, lanes] = parts[1][rows]
        lanes = slice(chunk * 1024, chunk * 1024 + 1024)
        for slot, held in enumerate((c_high, c_low)):
            sem = out_sems.at[2 * chunk + slot]
            outs.append(pltpu.make_async_copy(held.at[:, lanes], cand.at[slot, :, lanes], sem))
            outs[-1].start()
        high, low = c_high[:, lanes], c_low[:, lanes]
        top = product(high[0:256], high, (1, 1))
        bottom = product(high[256:512], high[256:512], (1, 1))
        both = product(high, low, (1, 1))
        if chunk == 0:
            same[0:256, :], same[256:512, 256:512], cross[...] = top, bottom, both
        else:
            same[0:256, :] += top
            same[256:512, 256:512] += bottom
            cross[...] += both

    if not second:
        copies[8].wait()
    spot = 0
    for a in range(4):
        for b in range(a, 4):
            rows, cols = slice(128 * a, 128 * a + 128), slice(128 * b, 128 * b + 128)
            total = same[rows, cols] + (cross[rows, cols] + cross[cols, rows].T)
            total = total * (1.0 / 524288)
            to = slice(128 * spot, 128 * spot + 128)
            packed[to, :] = total if second else total + added[to, :]
            spot += 1
    if second:
        outs.append(pltpu.make_async_copy(packed, grams[0].at[0:1280, :], out_sems.at[4]))
        outs[-1].start()
    else:
        for half in range(2):
            core = place[4] if half == 0 else 1 - place[4]
            grams[half][...] = packed[pl.ds(pl.multiple_of(core * 640, 640), 640), :]
    for copy in outs:
        copy.wait()


def transported(second, place, index, xfactor, mains, above, before, volume, upwind):
    part = jax.ShapeDtypeStruct((2, 512, WIDE), BF16)
    extra = [] if second else [*above, before]
    shapes = [(1280, 128)] if second else [(640, 128), (640, 128)]
    grams = [jax.ShapeDtypeStruct(shape, F32) for shape in shapes]
    return pl.pallas_call(
        functools.partial(transport_kernel, second),
        out_shape=(*grams, part),
        in_specs=[SMEM, SMEM, ANY] + [ANY] * 3 + ([] if second else [ANY] * 5) + [VMEM, VMEM],
        out_specs=(ANY, ANY) if second else (VMEM, VMEM, ANY),
        scratch_shapes=[
            pltpu.VMEM((4, 32, 2 * WIDE), F32),
            pltpu.VMEM((3, 256, 512), BF16),
            pltpu.VMEM((3, 256, 512), BF16),
            pltpu.VMEM((2 * TILES + 1, 128, 128), BF16),
            pltpu.VMEM((2 * TILES + 1, 128, 128), BF16),
            pltpu.VMEM((512, WIDE), BF16),
            pltpu.VMEM((512, WIDE), BF16),
            pltpu.VMEM((512, 512), F32),
            pltpu.VMEM((512, 512), F32),
            pltpu.VMEM((1280, 128), F32),
            pltpu.VMEM((1280, 128), F32),
            pltpu.SemaphoreType.DMA((9,)),
            pltpu.SemaphoreType.DMA((5,)),
        ],
        compiler_params=pltpu.CompilerParams(vmem_limit_bytes=50 << 20),
        cost_estimate=pl.CostEstimate(
            flops=9_000_000_000, bytes_accessed=8 << 20, transcendentals=0
        ),
        name="transport_second" if second else "transport_first",
    )(place, index, xfactor, *mains, *extra, volume, upwind)


def along_lanes(x, lane):
    return jnp.broadcast_to(x[:, lane : lane + 1], (8, 128))


def along_rows(x, row):
    return jnp.broadcast_to(x[row : row + 1, :], (8, 128))


def tree_sum(terms):
    while len(terms) > 1:
        terms = [sum(terms[i : i + 2][1:], terms[i]) for i in range(0, len(terms), 2)]
    return terms[0]


NEAR = 5


def factor_block(left, right, spread):
    row = lax.broadcasted_iota(jnp.int32, (8, 128), 0)
    left, right = list(left), list(right)
    upper, inverse = [], []

    def packed(lines):
        out = lines[0]
        for j in range(1, 8):
            out = jnp.where(row == j, lines[j], out)
        return out

    for step in range(16):
        near = min(16, step + 1 + NEAR)
        c = [[along_lanes(left[i], 8 * step + l) for l in range(8)] for i in range(step, near)]
        for l in range(8):
            spread[8 * step + l] = c[0][l]
        s = [
            [along_rows(spread[8 * step + l, i : i + 1, :], 0) if i >= l else None for l in range(8)]
            for i in range(8)
        ]
        lines = [[along_rows(left[step], l) for l in range(8)]]
        lines += [[along_rows(right[step], l) for l in range(8)]]
        lines += c[1:]
        for j in range(8):
            r = lax.rsqrt(s[j][j])
            for i in range(j + 1, 8):
                s[i][j] = s[i][j] * r
            for line in lines:
                line[j] = line[j] * r
            for l in range(j + 1, 8):
                for i in range(l, 8):
                    s[i][l] = s[i][l] - s[i][j] * s[l][j]
                for line in lines:
                    line[l] = line[l] - s[l][j] * line[j]
        wide_left, wide_right, *factors = lines
        upper.append(packed(wide_left))
        inverse.append(packed(wide_right))
        for i in range(step + 1, near):
            left[i] = left[i] - tree_sum([a * b for a, b in zip(factors[i - step - 1], wide_left)])
            right[i] = right[i] - tree_sum([a * b for a, b in zip(factors[i - step - 1], wide_right)])
        if near < 16:
            both = jnp.concatenate([upper[-1], inverse[-1]], axis=1)
            change = exact(upper[-1][:, 8 * near :], both, (0, 0))
            for i in range(near, 16):
                rows = slice(8 * (i - near), 8 * (i - near) + 8)
                left[i] = left[i] - change[rows, :128]
                right[i] = right[i] - change[rows, 128:]
    return upper, inverse


def factor_kernel(
    place, mine, other, coeffs, cand_first, cand_second, r_out, new_out,
    packed, work, spread, r_held, c_high, c_low, new, sems, out_sems,
):
    copies = []
    for side, cand in enumerate((cand_first, cand_second)):
        lanes = slice(side * WIDE, side * WIDE + WIDE)
        for slot, held in enumerate((c_high, c_low)):
            sem = sems.at[2 * side + slot]
            copies.append(pltpu.make_async_copy(cand.at[slot], held.at[:, lanes], sem))
    for copy in copies:
        copy.start()
    packed[pl.ds(pl.multiple_of(place[0] * 640, 640), 640), :] = mine[...]
    packed[pl.ds(pl.multiple_of((1 - place[0]) * 640, 640), 640), :] = other[...]
    row = lax.broadcasted_iota(jnp.int32, (128, 128), 0)
    col = lax.broadcasted_iota(jnp.int32, (128, 128), 1)
    eye = (row == col).astype(F32)
    zero = jnp.zeros((128, 128), F32)
    at = [slice(128 * a, 128 * a + 128) for a in range(4)]
    beside = [slice(512 + 128 * a, 640 + 128 * a) for a in range(4)]
    spot = 0
    for a in range(4):
        for b in range(4):
            work[at[a], beside[b]] = eye if a == b else zero
            if b >= a:
                work[at[a], at[b]] = packed[128 * spot : 128 * spot + 128, :]
                spot += 1
            else:
                r_held[at[a], at[b]] = zero
    for a in range(4):
        first = 128 * a
        upper, inverse = factor_block(
            [work[first + 8 * i : first + 8 * i + 8, at[a]] for i in range(16)],
            [eye[8 * i : 8 * i + 8] for i in range(16)],
            spread.at[a],
        )
        diag = jnp.where(row >= col, jnp.concatenate(inverse, axis=0), 0.0)
        r_held[at[a], at[a]] = jnp.where(row <= col, jnp.concatenate(upper, axis=0), 0.0)
        work[at[a], beside[a]] = diag
        if a:
            done = slice(512, 512 + first)
            work[at[a], done] = exact(diag, work[at[a], done], (1, 0))
        if a < 3:
            rest = exact(diag, work[at[a], first + 128 : 512], (1, 0))
            r_held[at[a], first + 128 : 512] = rest
            for b in range(a + 1, 4):
                part = rest[:, 128 * (b - a - 1) : 128 * (b - a)]
                right = slice(128 * b, 512)
                work[at[b], right] -= exact(part, rest[:, 128 * (b - a - 1) :], (0, 0))
                done = slice(512, 512 + first + 128)
                work[at[b], done] -= exact(part, work[at[a], done], (0, 0))
    outs = [pltpu.make_async_copy(r_held, r_out, out_sems.at[4])]
    outs[0].start()
    weight_high, weight_low = halves(exact(coeffs[...], work[:, 512:1024], (0, 0)))
    weights = jnp.concatenate([weight_high, weight_low], axis=0)
    for copy in copies:
        copy.wait()
    for chunk in range(4):
        lanes = slice(chunk * 1024, chunk * 1024 + 1024)
        both = product(weights, c_high[:, lanes], (1, 0))
        low = product(weight_high, c_low[:, lanes], (1, 0))
        new[:, lanes] = both[0:128] + (both[128:256] + low)
        outs.append(pltpu.make_async_copy(new.at[:, lanes], new_out.at[:, lanes], out_sems.at[chunk]))
        outs[-1].start()
    for copy in outs:
        copy.wait()


def factored(place, mine, other, coeffs, cand_first, cand_second):
    return pl.pallas_call(
        factor_kernel,
        out_shape=(
            jax.ShapeDtypeStruct((512, 512), F32),
            jax.ShapeDtypeStruct((128, 2 * WIDE), F32),
        ),
        in_specs=[SMEM, VMEM, VMEM, VMEM, ANY, ANY],
        out_specs=(ANY, ANY),
        scratch_shapes=[
            pltpu.VMEM((1280, 128), F32),
            pltpu.VMEM((512, 1024), F32),
            pltpu.VMEM((4, 128, 8, 128), F32),
            pltpu.VMEM((512, 512), F32),
            pltpu.VMEM((512, 2 * WIDE), BF16),
            pltpu.VMEM((512, 2 * WIDE), BF16),
            pltpu.VMEM((128, 2 * WIDE), F32),
            pltpu.SemaphoreType.DMA((4,)),
            pltpu.SemaphoreType.DMA((5,)),
        ],
        compiler_params=pltpu.CompilerParams(vmem_limit_bytes=52 << 20),
        name="factor",
    )(place, mine, other, coeffs, cand_first, cand_second)


def sent(value, axis, by):
    count = lax.axis_size(axis)
    return lax.ppermute(value, axis, [(i, (i + by) % count) for i in range(count)])


def pieces_from_here(value, axis):
    count, here = lax.axis_size(axis), lax.axis_index(axis)
    split = value.reshape(count, -1, value.shape[-1])
    return [
        lax.dynamic_index_in_dim(split, (here + by) % count, 0, keepdims=False)
        for by in range(count)
    ]


def scattered_sum(value, axis):
    pieces = pieces_from_here(value, axis)
    two, one, three = (sent(pieces[by], axis, by) for by in (2, 1, 3))
    return (pieces[0] + two) + (one + three)


def exchanged_sum(value, axis):
    three, two, one = (sent(value, axis, by) for by in (3, 2, 1))
    return (three + one) + (two + value)


def gathered(value, axis):
    count, here = lax.axis_size(axis), lax.axis_index(axis)
    out = jnp.zeros((count, *value.shape), value.dtype)
    for by in (0, 3, 2, 1):
        part = sent(value, axis, by) if by else value
        out = lax.dynamic_update_index_in_dim(out, part, (here - by) % count, 0)
    return out.reshape(-1, value.shape[-1])


def summed(keep, send):
    part = scattered_sum(keep + sent(send, "core", 1), "x")
    part = exchanged_sum(exchanged_sum(part, "y"), "rank")
    mine = gathered(part, "x")
    return mine, sent(mine, "core", 1)


def tile_index(neighbor, first):
    at = neighbor - first
    odd_place = jnp.arange(neighbor.shape[1]) % 2
    tile = jnp.where(at % 2 == odd_place, at // 2, TILES + (at + 1) // 2)
    return jnp.where(neighbor >= 0, tile, ZERO_TILE).astype(jnp.int32)


def shards(xfactor, volume, upwind, neighbor, coeffs):
    sub_elems = neighbor.shape[1] // 4
    rank = lax.axis_index("rank")
    count = lax.axis_size(SPACE)
    above = xfactor[:, 7 * WIDE :]
    above = lax.ppermute(above, SPACE, [(i, i + 1) for i in range(count - 1)])
    order = (2, 1, 3)
    mains, halos = [], []
    for by in order:
        to = (rank + by) % 4
        piece = lax.dynamic_slice_in_dim(xfactor, to * 2 * WIDE, 2 * WIDE, 1)
        mains.append(sent(piece, "rank", by))
    for by in (0, *order):
        to = (rank + by) % 4
        inside = lax.dynamic_slice_in_dim(xfactor, jnp.maximum((2 * to - 1) * WIDE, 0), WIDE, 1)
        piece = jnp.where(to == 0, above, inside)
        halos.append(sent(piece, "rank", by) if by else piece)
    core = lax.axis_index("core")
    place = jnp.stack([(rank - by) % 4 for by in (0, *order)] + [core]).astype(jnp.int32)
    first = (lax.axis_index(SPACE) * 4 + rank) * sub_elems
    own = lax.dynamic_slice_in_dim(neighbor, rank * sub_elems, sub_elems, 1)
    index_first = tile_index(own[:, :HALO_EL], first - HALO_EL)
    index_second = tile_index(own[:, HALO_EL:], first)
    before, second = transported(
        True, place, index_second, xfactor, mains, None, None, volume, upwind
    )
    keep, send, start = transported(
        False, place, index_first, xfactor, mains, halos, before, volume, upwind
    )
    mine, other = summed(keep, send)
    r_factor, new_factor = factored(place[4:], mine, other, coeffs, start, second)
    return new_factor, r_factor


def solution(mesh):
    finer = Mesh(mesh.devices.reshape(4, 4, 2, 4), SPACE_RANK)
    placed = (P("rank", SPACE), P(), P(), P(None, SPACE), P())
    return jax.shard_map(
        shards, mesh=finer, in_specs=placed, out_specs=(P(None, SPACE_RANK), P()), check_vma=False
    )
```
